256 devices in a mesh: dp: 8 (over y, core), row: 2 (over x_lo), col: 16 (over z, x_hi).
Axes of the slice: x: 4 (x_hi: 2, x_lo: 2; x = x_hi * 2 + x_lo), y: 4, z: 8, core: 2. Of those that a mesh axis runs over, the one named last changes fastest.
Arguments:
- activations: bfloat16 [4096, 53248], P('dp', ('row', 'col')), may hold values from -6 to 6
- weights: bfloat16 [53248, 8192], P(('row', 'col'), 'dp'), may hold values from -6 to 6
- codes: int32 [1024, 8192], P(None, 'dp'), may hold values from 0 to 15
- scale_index: int32 [8, 8192], P(None, 'dp'), may hold values from 0 to 15
- scale_table: float32 [16], replicated, may hold values from 0.1 to 0.3
- inverse_block: float32 [1024, 1024], P(('row', 'col')), may hold values from -0.1875 to 0.1875
- block_index: int32 [1], replicated, may hold values from 0 to 25
Outputs:
- updated: bfloat16 [53248, 8192], P(('row', 'col'), 'dp')
The draws below stay inside these ranges and needn't reach their ends.
All inputs are finite; a program needn't handle non-finite values.
Results may differ from the reference program's by a relative error of at most 0.001.
Values may be sent and summed in bfloat16 or wider, within the bound.
No kernel may reach another device: no remote copies, remote signals or barrier semaphores. Data moves between devices by JAX's collectives and lax.ppermute only.
A program may use at most 128 MiB of HBM per device.

```python
import math
import jax
import jax.numpy as jnp
from jax import lax

KIN = 53248
OUT = 8192
BLK = 1024
GROUP = 128
LEVELS = 16
TOKENS = 4096


def touch_ends(entries, rng, smallest, top_value):
    longest = entries.shape.index(max(entries.shape))
    spots = []
    for shift in (0, 1):
        where = [jax.random.randint(jax.random.fold_in(rng, axis), (), 0, length) for axis, length in enumerate(entries.shape)]
        where[longest] = (where[longest] + shift) % entries.shape[longest]
        spots.append(tuple(where))
    return entries.at[spots[0]].set(smallest).at[spots[1]].set(top_value)


def steps_of(rng, dims, split, least, high):
    loudness = 1.0
    for position, blocks in split:
        heights = jax.random.uniform(jax.random.fold_in(jax.random.fold_in(rng, 6), position), (blocks,), jnp.float32, least / len(split), high / len(split))
        loudness = loudness * jnp.repeat(jnp.exp(heights), dims[position] // blocks).reshape((-1,) + (1,) * (len(dims) - 1 - position))
    return loudness


def noise(own_key, extent, width, bound, shards=(), kind=jnp.bfloat16):
    loudness = steps_of(own_key, extent, shards, -0.22, 0.18) if shards else 1.0
    array = jax.random.normal(own_key, extent, jnp.float32) * width * loudness
    return jnp.minimum(jnp.maximum(array, -bound), bound).astype(kind)


def setup_inputs(seed: int = 0) -> dict:
    streams_of = jax.random.split(jax.random.key(seed), 8)
    activations = noise(streams_of[0], (TOKENS, KIN), 1.0, 6.0, ((0, 8), (1, 32)))
    weights = noise(streams_of[1], (KIN, OUT), 1.0, 6.0, ((0, 32), (1, 8)))
    codes = touch_ends(jax.random.randint(streams_of[2], (BLK, OUT), 0, 16), jax.random.fold_in(streams_of[2], 1), 0, 15).astype(jnp.int32)
    scale_index = touch_ends(jax.random.randint(streams_of[3], (BLK // GROUP, OUT), 0, LEVELS), jax.random.fold_in(streams_of[3], 1), 0, LEVELS - 1).astype(jnp.int32)
    scale_table = jnp.clip(jnp.exp(jax.random.uniform(streams_of[4], (LEVELS,), jnp.float32, math.log(0.1), math.log(0.3))), 0.1, 0.3)
    inverse_block = noise(streams_of[5], (BLK, BLK), BLK ** -0.5, 0.1875, ((0, 32),), jnp.float32)
    block_index = jax.random.randint(streams_of[6], (1,), 0, KIN // BLK // 2).astype(jnp.int32)
    return dict(activations=activations, weights=weights, codes=codes, scale_index=scale_index, scale_table=scale_table, inverse_block=inverse_block, block_index=block_index)


def reference(activations, weights, codes, scale_index, scale_table, inverse_block, block_index):
    first_row = block_index[0].astype(jnp.int32) * BLK
    x_block = lax.dynamic_slice_in_dim(activations, first_row, BLK, 1)
    w_block = lax.dynamic_slice_in_dim(weights, first_row, BLK, 0)
    chosen = (scale_index[:, :, None] == jnp.arange(LEVELS, dtype=jnp.int32)).astype(jnp.float32)
    group_scale = jnp.sum(chosen * scale_table.astype(jnp.float32), axis=2)
    scale_rows = jnp.repeat(group_scale, GROUP, axis=0)
    quantized = scale_rows * (codes.astype(jnp.float32) - 7.5)
    deviation = w_block.astype(jnp.float32) - quantized
    block_error = jnp.dot(inverse_block, deviation, precision=lax.Precision.HIGHEST)
    hessian_panel = lax.dot_general(activations, x_block, (((0,), (0,)), ((), ())), preferred_element_type=jnp.float32) * (2.0 / TOKENS)
    update = jnp.dot(hessian_panel, block_error, precision=lax.Precision.HIGHEST)
    row_ids = jnp.arange(KIN, dtype=jnp.int32)[:, None]
    kept_values = weights.astype(jnp.float32)
    quant_full = lax.dynamic_update_slice_in_dim(jnp.zeros((KIN, OUT), jnp.float32), quantized, first_row, 0)
    result = jnp.where(row_ids >= first_row + BLK, kept_values - update, kept_values)
    result = jnp.where((row_ids >= first_row) & (row_ids < first_row + BLK), quant_full, result)
    return result.astype(jnp.bfloat16)
```

```python
import functools
import jax
import jax.numpy as jnp
from jax import lax
from jax.experimental import pallas as pl
from jax.experimental.pallas import tpu as pltpu
from jax.sharding import Mesh, PartitionSpec as P

BLK = 1024
GROUP = 128
LEVELS = 16
UNIT = 128
UNITS = BLK // UNIT
STEPS_PER_OCTAVE = 128.0
F32, BF16, S16 = jnp.float32, jnp.bfloat16, jnp.int16
PLANE = ("xl", "z", "xh")


def tile_at(x, z):
    return (x % 2) * 16 + (z % 8) * 2 + (x % 4) // 2


def ring(axis, size, shift, value):
    return lax.ppermute(value, axis, [(i, (i + shift) % size) for i in range(size)])


def pick_kernel(index, x_ref, w_ref, x_out, w_out):
    x_out[...] = x_ref[...].reshape(4, 128, UNIT)
    w = w_ref[...]
    for p in range(4):
        w_out[p] = w[:, 256 * p : 256 * (p + 1)]


def pick_units(activations, weights, index):
    tokens, cols = activations.shape[0], weights.shape[1]
    return pl.pallas_call(
        pick_kernel,
        grid_spec=pltpu.PrefetchScalarGridSpec(
            num_scalar_prefetch=1,
            grid=(UNITS,),
            in_specs=[
                pl.BlockSpec((tokens, UNIT), lambda j, u: (0, u[j])),
                pl.BlockSpec((UNIT, cols), lambda j, u: (u[j], 0)),
            ],
            out_specs=[
                pl.BlockSpec((4, 128, UNIT), lambda j, u: (0, 0, j)),
                pl.BlockSpec((4, UNIT, 256), lambda j, u: (0, j, 0)),
            ],
        ),
        out_shape=[
            jax.ShapeDtypeStruct((4, 128, BLK), BF16),
            jax.ShapeDtypeStruct((4, BLK, 256), BF16),
        ],
        name="pick_units",
    )(index, activations, weights)


def scatter_x(pieces, x, xh, from_low):
    def to(shift):
        pairs = [(tile_at(s, z), tile_at(s + shift, z)) for s in (0, 2) for z in range(8)]
        return lax.ppermute(
            lax.dynamic_index_in_dim(pieces, (2 * xh + shift) % 4, 0, False), PLANE, pairs
        )

    up, down, across = to(1), to(3), to(2)
    even = x % 2 == 0
    own = lax.dynamic_index_in_dim(pieces, x, 0, False)
    near = jnp.where(even, own, up)
    far = jnp.where(even, across, down)
    return jnp.where(from_low, near, far)


def spread_z(piece, distance):
    up, down = ring("z", 8, 3, piece), ring("z", 8, -3, piece)
    piece = jnp.where(distance == 3, up, jnp.where(distance == 5, down, piece))
    up, down = ring("z", 8, 1, piece), ring("z", 8, -1, piece)
    from_below = (distance == 1) | (distance == 4) | (distance == 6)
    from_above = (distance == 7) | (distance == 2)
    return jnp.where(from_below, up, jnp.where(from_above, down, piece))


def quantize(values):
    rows = values.shape[-2]
    top = jnp.max(jnp.abs(values), axis=-1, keepdims=True)
    level = jnp.floor(jnp.log2(32700.0 / jnp.maximum(top, 1e-25)) * STEPS_PER_OCTAVE)
    scaled = jnp.round(values * jnp.exp2(level / STEPS_PER_OCTAVE)).astype(jnp.int32).astype(S16)
    levels = jnp.swapaxes(level, -1, -2).astype(jnp.int32).astype(S16)
    widths = [(0, 0)] * (values.ndim - 2) + [(0, 15), (0, values.shape[-1] - rows)]
    return jnp.concatenate([scaled, jnp.pad(levels, widths)], axis=-2)


def scales_of(message):
    rows = message.shape[-2] - 16
    level = message[..., rows : rows + 1, :rows].astype(F32)
    return jnp.swapaxes(jnp.exp2(-level / STEPS_PER_OCTAVE), -1, -2)


def dequantize(message):
    return message[..., :-16, :].astype(F32) * scales_of(message)


def split(values):
    high = values.astype(BF16)
    return high, (values - high.astype(F32)).astype(BF16)


def mm(a, b):
    return jnp.dot(a, b, preferred_element_type=F32)


def error_kernel(inv_ref, w_ref, q_ref, high_ref, low_ref):
    inv_high, inv_low = split(inv_ref[...])
    dev_high, dev_low = split(w_ref[...].astype(F32) - q_ref[...])
    error = mm(inv_high, dev_high) + (mm(inv_high, dev_low) + mm(inv_low, dev_high))
    high_ref[...], low_ref[...] = split(error)


def block_error(inverse, w_block, quantized):
    cols, wide = w_block.shape[1], 256
    stripe = pl.BlockSpec((BLK, wide), lambda i: (0, i))
    return pl.pallas_call(
        error_kernel,
        grid=(cols // wide,),
        in_specs=[pl.BlockSpec((BLK, BLK), lambda i: (0, 0)), stripe, stripe],
        out_specs=[stripe, stripe],
        out_shape=[jax.ShapeDtypeStruct((BLK, cols), BF16)] * 2,
        compiler_params=pltpu.CompilerParams(vmem_limit_bytes=40 << 20),
        cost_estimate=pl.CostEstimate(
            flops=6 * BLK * BLK * cols, bytes_accessed=BLK * cols * 14, transcendentals=0
        ),
        name="block_error",
    )(inverse, w_block, quantized)


def update_kernel(start_ref, h_ref, scale_ref, high_ref, low_ref, base_ref, out_ref):
    rows = out_ref.shape[0]
    h = h_ref[0, 0, :rows].astype(jnp.int32).astype(F32)
    h_high, h_low = split(h)
    update = mm(h_high, high_ref[...]) + (mm(h_high, low_ref[...]) + mm(h_low, high_ref[...]))
    base = base_ref[...].astype(F32)
    row = lax.broadcasted_iota(jnp.int32, base.shape, 0) + pl.program_id(0) * rows
    result = jnp.where(row >= start_ref[0], base - update * scale_ref[0, 0], base)
    out_ref[...] = result.astype(BF16)


def apply_update(start, panel, scales, high, low, base):
    rows, cols = panel.shape[2] - 16, base.shape[1]
    whole = pl.BlockSpec((BLK, cols), lambda i, s: (0, 0))
    stripe = pl.BlockSpec((rows, cols), lambda i, s: (i, 0))
    return pl.pallas_call(
        update_kernel,
        grid_spec=pltpu.PrefetchScalarGridSpec(
            num_scalar_prefetch=1,
            grid=(base.shape[0] // rows,),
            in_specs=[
                pl.BlockSpec((1, 1, rows + 16, BLK), lambda i, s: (i % 4, i // 4, 0, 0)),
                pl.BlockSpec((1, 1, rows, 1), lambda i, s: (i % 4, i // 4, 0, 0)),
                whole,
                whole,
                stripe,
            ],
            out_specs=stripe,
        ),
        out_shape=jax.ShapeDtypeStruct(base.shape, BF16),
        compiler_params=pltpu.CompilerParams(vmem_limit_bytes=40 << 20),
        cost_estimate=pl.CostEstimate(
            flops=6 * base.shape[0] * BLK * cols,
            bytes_accessed=base.shape[0] * cols * 6 + BLK * cols * 4,
            transcendentals=0,
        ),
        name="apply_update",
    )(start, panel, scales, high, low, base)


def local(activations, weights, codes, scale_index, scale_table, inverse_block, block_index):
    y, core = lax.axis_index("y"), lax.axis_index("core")
    xl, z, xh = (lax.axis_index(a) for a in PLANE)
    x = 2 * xh + xl
    tile = lax.axis_index(PLANE)
    shard_rows = weights.shape[0]
    tile_units = shard_rows // UNIT
    token_total = activations.shape[0] * 8
    first_unit = block_index[0] * UNITS
    units = first_unit + jnp.arange(UNITS, dtype=jnp.int32)
    owner = units // tile_units
    x_owner, z_owner = 2 * (owner % 2), (owner // 2) % 8
    distance = (z - z_owner) % 8
    from_low = x_owner == jnp.where(x % 2 == 0, x, (x + 3) % 4)

    own_rows = inverse_block.shape[0] // 2
    inverse_part = lax.dynamic_slice_in_dim(inverse_block, core * own_rows, own_rows, 0)
    inverse = lax.all_gather(inverse_part, ("xh", "xl", "z", "core"), axis=0)
    inverse = inverse.reshape(2, 2, 8, 2, own_rows, BLK).transpose(1, 2, 0, 3, 4, 5)
    inverse = inverse.reshape(BLK, BLK)

    index = jnp.clip(units - tile * tile_units, 0, tile_units - 1)
    x_pieces, w_pieces = pick_units(activations, weights, index)

    half = shard_rows // 2
    x_mine = lax.dynamic_slice_in_dim(activations, core * half, half, 1)
    x_theirs = lax.dynamic_slice_in_dim(activations, (1 - core) * half, half, 1)
    x_other = ring("core", 2, 1, x_theirs)
    x_low = jnp.where(core == 0, x_mine, x_other).reshape(4, 128, half)
    x_high = jnp.where(core == 0, x_other, x_mine).reshape(4, 128, half)
    x_rows = jnp.stack([x_low, x_high], axis=1).reshape(1024, half)

    lanes = lambda v: jnp.repeat(v, UNIT)[None, :]
    sublanes = lambda v: jnp.repeat(v, UNIT)[:, None]
    x_piece = scatter_x(x_pieces, x, xh, lanes(from_low))
    x_piece, w_pieces = lax.optimization_barrier((x_piece, w_pieces))
    w_piece = scatter_x(w_pieces, x, xh, sublanes(from_low))
    x_piece = spread_z(x_piece, lanes(distance))
    x_piece, w_piece = lax.optimization_barrier((x_piece, w_piece))
    w_piece = spread_z(w_piece, sublanes(distance))

    x_block = lax.all_gather(
        x_piece.astype(jnp.float16), ("xh", "xl", "core"), axis=0, tiled=True
    ).astype(BF16)

    partial_panel = lax.dot_general(
        x_rows, x_block, (((0,), (0,)), ((), ())), preferred_element_type=F32
    )
    quarter = half // 4
    parts = partial_panel.reshape(4, quarter, BLK)
    message = quantize(parts)
    total = lax.dynamic_index_in_dim(parts, y, 0, False)
    for shift in (1, 3, 2):
        sent = lax.dynamic_index_in_dim(message, (y + shift) % 4, 0, False)
        total = total + dequantize(ring("y", 4, shift, sent))
    panel = lax.all_gather(quantize(total), ("y", "core"), axis=0)
    panel = panel.reshape(4, 2, quarter + 16, BLK)
    scales = scales_of(panel) * (2.0 / token_total)

    chosen = (scale_index[:, :, None] == jnp.arange(LEVELS, dtype=jnp.int32)).astype(F32)
    group_scale = jnp.sum(chosen * scale_table, axis=2)
    quantized = jnp.repeat(group_scale, GROUP, axis=0) * (codes.astype(F32) - 7.5)

    w_all = lax.all_gather(w_piece.astype(jnp.float16), ("xh", "xl"), axis=0)
    w_block = w_all.transpose(1, 0, 2).reshape(BLK, 1024).astype(BF16)
    high, low = block_error(inverse, w_block, quantized)

    first_local = block_index[0] * BLK - tile * shard_rows
    padded = jnp.pad(quantized.astype(BF16), [(shard_rows, shard_rows), (0, 0)])
    begin = jnp.clip(shard_rows - first_local, 0, BLK + shard_rows)
    quant_rows = lax.dynamic_slice_in_dim(padded, begin, shard_rows, 0)
    row = jnp.arange(shard_rows, dtype=jnp.int32)[:, None] - first_local
    base = jnp.where((row >= 0) & (row < BLK), quant_rows, weights)
    start = (first_local + BLK).reshape(1)
    return apply_update(start, panel, scales, high, low, base)


def solution(mesh):
    cube = Mesh(mesh.devices.reshape(4, 2, 2, 8, 2), ("y", "core") + PLANE)
    return jax.shard_map(
        local,
        mesh=cube,
        in_specs=(
            P(("y", "core"), PLANE),
            P(PLANE, ("y", "core")),
            P(None, ("y", "core")),
            P(None, ("y", "core")),
            P(),
            P(PLANE, None),
            P(),
        ),
        out_specs=P(PLANE, ("y", "core")),
        check_vma=False,
    )
```

```python
import functools
import jax
import jax.numpy as jnp
from jax import lax
from jax.experimental import pallas as pl
from jax.experimental.pallas import tpu as pltpu
from jax.sharding import Mesh, PartitionSpec as P

BLK = 1024
GROUP = 128
LEVELS = 16
UNIT = 128
UNITS = BLK // UNIT
STEPS_PER_OCTAVE = 128.0
F32, BF16, S16 = jnp.float32, jnp.bfloat16, jnp.int16
PLANE = ("xl", "z", "xh")


def tile_at(x, z):
    return (x % 2) * 16 + (z % 8) * 2 + (x % 4) // 2


def ring(axis, size, shift, value):
    return lax.ppermute(value, axis, [(i, (i + shift) % size) for i in range(size)])


def pick_kernel(rows, cols, scalars, src_ref, *out_refs):
    x = scalars[UNITS]
    for k, out_ref in enumerate(out_refs):
        p = (x + k) % 4
        if rows is not None:
            out_ref[...] = src_ref[pl.ds(pl.multiple_of(p * rows, rows), rows), :]
        else:
            out_ref[...] = src_ref[:, pl.ds(pl.multiple_of(p * cols, cols), cols)]


def pick(source, along, scalars, name):
    other = source.shape[1 - along]
    part = other // 4
    if along == 1:
        in_spec = pl.BlockSpec((other, UNIT), lambda j, u: (0, u[j]))
        out_spec = pl.BlockSpec((part, UNIT), lambda j, u: (0, j))
        shape, rows, cols = (part, BLK), part, None
    else:
        in_spec = pl.BlockSpec((UNIT, other), lambda j, u: (u[j], 0))
        out_spec = pl.BlockSpec((UNIT, part), lambda j, u: (j, 0))
        shape, rows, cols = (BLK, part), None, part
    return pl.pallas_call(
        functools.partial(pick_kernel, rows, cols),
        grid_spec=pltpu.PrefetchScalarGridSpec(
            num_scalar_prefetch=1, grid=(UNITS,), in_specs=[in_spec], out_specs=[out_spec] * 4
        ),
        out_shape=[jax.ShapeDtypeStruct(shape, BF16)] * 4,
        name=name,
    )(scalars, source)


def plane_pairs(columns, shift):
    return [(tile_at(s, z), tile_at(s + shift, z)) for s in columns for z in range(8)]


def scatter_x(pieces, x, from_low):
    own, *others = pieces
    up, across, down = (
        lax.ppermute(piece, PLANE, plane_pairs((0, 2), shift))
        for shift, piece in zip((1, 2, 3), others)
    )
    even = x % 2 == 0
    near = jnp.where(even, own, up)
    far = jnp.where(even, across, down)
    return jnp.where(from_low, near, far)


def spread_z(piece, distance, beside=None):
    up, down = ring("z", 8, 3, piece), ring("z", 8, -3, piece)
    if beside is not None:
        up, down, beside = lax.optimization_barrier((up, down, beside))
    piece = jnp.where(distance == 3, up, jnp.where(distance == 5, down, piece))
    up, down = ring("z", 8, 1, piece), ring("z", 8, -1, piece)
    from_below = (distance == 1) | (distance == 4) | (distance == 6)
    from_above = (distance == 7) | (distance == 2)
    return jnp.where(from_below, up, jnp.where(from_above, down, piece)), beside


def quantize(values):
    rows = values.shape[-2]
    top = jnp.max(jnp.abs(values), axis=-1, keepdims=True)
    level = jnp.floor(jnp.log2(32700.0 / jnp.maximum(top, 1e-25)) * STEPS_PER_OCTAVE)
    scaled = jnp.round(values * jnp.exp2(level / STEPS_PER_OCTAVE)).astype(jnp.int32).astype(S16)
    levels = jnp.swapaxes(level, -1, -2).astype(jnp.int32).astype(S16)
    widths = [(0, 0)] * (values.ndim - 2) + [(0, 15), (0, values.shape[-1] - rows)]
    return jnp.concatenate([scaled, jnp.pad(levels, widths)], axis=-2)


def scales_of(message):
    rows = message.shape[-2] - 16
    level = message[..., rows : rows + 1, :rows].astype(F32)
    return jnp.swapaxes(jnp.exp2(-level / STEPS_PER_OCTAVE), -1, -2)


def dequantize(message):
    return message[..., :-16, :].astype(F32) * scales_of(message)


def split(values):
    high = values.astype(BF16)
    return high, (values - high.astype(F32)).astype(BF16)


def mm(a, b):
    return jnp.dot(a, b, preferred_element_type=F32)


def error_kernel(inv_ref, w_ref, q_ref, out_ref):
    inv_high, inv_low = split(inv_ref[...])
    dev_high, dev_low = split(w_ref[...].astype(F32) - q_ref[...])
    error = mm(inv_high, dev_high) + (mm(inv_high, dev_low) + mm(inv_low, dev_high))
    i = pl.program_id(0)
    first = ((i % 2) * 16 + i // 2) * 32
    for z in range(8):
        at = pl.multiple_of(first + z * 64, 32)
        out_ref[pl.ds(at, 32), :] = error[z * 32 : (z + 1) * 32]


def block_error(inverse, w_piece, quantized):
    wide = w_piece.shape[1]
    whole = pl.BlockSpec((BLK, wide), lambda i: (0, 0))
    return pl.pallas_call(
        error_kernel,
        grid=(4,),
        in_specs=[pl.BlockSpec((BLK // 4, BLK), lambda i: (i, 0)), whole, whole],
        out_specs=whole,
        out_shape=jax.ShapeDtypeStruct((BLK, wide), F32),
        compiler_params=pltpu.CompilerParams(vmem_limit_bytes=32 << 20),
        cost_estimate=pl.CostEstimate(
            flops=6 * BLK * BLK * wide, bytes_accessed=BLK * BLK * 4, transcendentals=0
        ),
        name="block_error",
    )(inverse, w_piece, quantized)


def quantize_columns(error):
    top = jnp.max(jnp.abs(error), axis=0, keepdims=True)
    level = jnp.floor(jnp.log2(32700.0 / jnp.maximum(top, 1e-25)) * STEPS_PER_OCTAVE)
    scaled = jnp.round(error * jnp.exp2(level / STEPS_PER_OCTAVE))
    levels = jnp.broadcast_to(level, (16, error.shape[1]))
    return jnp.concatenate([scaled, levels], axis=0).astype(jnp.int32).astype(S16)


def update_kernel(scalars, h_ref, scale_ref, e0, e1, e2, e3, base_ref, out_ref, high_ref, low_ref, factor_ref):
    rows, wide = out_ref.shape[0], e0.shape[1]

    @pl.when(pl.program_id(0) == 0)
    def _():
        for k, e in enumerate((e0, e1, e2, e3)):
            high_ref[k], low_ref[k] = split(e[:BLK].astype(jnp.int32).astype(F32))
            level = e[BLK : BLK + 16].astype(jnp.int32).astype(F32)
            factor_ref[k] = jnp.exp2(level * (-1.0 / STEPS_PER_OCTAVE))

    h_high, h_low = split(h_ref[0, 0, :rows].astype(jnp.int32).astype(F32))
    row = lax.broadcasted_iota(jnp.int32, (rows, wide), 0) + pl.program_id(0) * rows
    for k in range(4):
        cols = pl.ds(pl.multiple_of(((scalars[1] + 4 - k) % 4) * wide, wide), wide)
        update = mm(h_high, high_ref[k]) + (mm(h_high, low_ref[k]) + mm(h_low, high_ref[k]))
        update = update * scale_ref[0, 0] * factor_ref[k, 0:1]
        base = base_ref[:, cols].astype(F32)
        out_ref[:, cols] = jnp.where(row >= scalars[0], base - update, base).astype(BF16)


def apply_update(scalars, panel, scales, errors, base):
    rows, cols = panel.shape[2] - 16, base.shape[1]
    wide = cols // 4
    whole = pl.BlockSpec((BLK + 16, wide), lambda i, s: (0, 0))
    stripe = pl.BlockSpec((rows, cols), lambda i, s: (i, 0))
    return pl.pallas_call(
        update_kernel,
        grid_spec=pltpu.PrefetchScalarGridSpec(
            num_scalar_prefetch=1,
            grid=(base.shape[0] // rows,),
            in_specs=[
                pl.BlockSpec((1, 1, rows + 16, BLK), lambda i, s: (i % 4, i // 4, 0, 0)),
                pl.BlockSpec((1, 1, rows, 1), lambda i, s: (i % 4, i // 4, 0, 0)),
                whole,
                whole,
                whole,
                whole,
                stripe,
            ],
            out_specs=stripe,
            scratch_shapes=[
                pltpu.VMEM((4, BLK, wide), BF16),
                pltpu.VMEM((4, BLK, wide), BF16),
                pltpu.VMEM((4, 16, wide), F32),
            ],
        ),
        out_shape=jax.ShapeDtypeStruct(base.shape, BF16),
        compiler_params=pltpu.CompilerParams(vmem_limit_bytes=32 << 20),
        cost_estimate=pl.CostEstimate(
            flops=6 * base.shape[0] * BLK * cols,
            bytes_accessed=base.shape[0] * cols * 6 + BLK * cols * 2,
            transcendentals=0,
        ),
        name="apply_update",
    )(scalars, panel, scales, *errors, base)


def local(activations, weights, codes, scale_index, scale_table, inverse_block, block_index):
    y, core = lax.axis_index("y"), lax.axis_index("core")
    xl, z, xh = (lax.axis_index(a) for a in PLANE)
    x = 2 * xh + xl
    tile = lax.axis_index(PLANE)
    shard_rows = weights.shape[0]
    tile_units = shard_rows // UNIT
    token_total = activations.shape[0] * 8
    first_unit = block_index[0] * UNITS
    units = first_unit + jnp.arange(UNITS, dtype=jnp.int32)
    owner = units // tile_units
    x_owner, z_owner = 2 * (owner % 2), (owner // 2) % 8
    distance = (z - z_owner) % 8
    from_low = x_owner == jnp.where(x % 2 == 0, x, (x + 3) % 4)

    own_rows = inverse_block.shape[0] // 2
    inverse_part = lax.dynamic_slice_in_dim(inverse_block, core * own_rows, own_rows, 0)
    inverse = lax.all_gather(inverse_part, ("xh", "xl", "z", "core"), axis=0)
    inverse = inverse.reshape(BLK, BLK)

    index = jnp.clip(units - tile * tile_units, 0, tile_units - 1)
    picks = jnp.append(index, x)
    x_pieces = pick(activations, 1, picks, "pick_columns")
    w_pieces = pick(weights, 0, picks, "pick_rows")

    half = shard_rows // 2
    x_mine = lax.dynamic_slice_in_dim(activations, core * half, half, 1)
    x_theirs = lax.dynamic_slice_in_dim(activations, (1 - core) * half, half, 1)
    x_other = ring("core", 2, 1, x_theirs)
    x_low = jnp.where(core == 0, x_mine, x_other).reshape(4, 128, half)
    x_high = jnp.where(core == 0, x_other, x_mine).reshape(4, 128, half)
    x_rows = jnp.stack([x_low, x_high], axis=1).reshape(1024, half).T

    lanes = lambda v: jnp.repeat(v, UNIT)[None, :]
    sublanes = lambda v: jnp.repeat(v, UNIT)[:, None]
    x_piece = scatter_x(x_pieces, x, lanes(from_low))
    x_piece, w_pieces = lax.optimization_barrier((x_piece, w_pieces))
    w_piece = scatter_x(w_pieces, x, sublanes(from_low))
    x_piece, x_rows = spread_z(x_piece, lanes(distance), x_rows)
    x_piece, w_piece = lax.optimization_barrier((x_piece, w_piece))
    w_piece, _ = spread_z(w_piece, sublanes(distance))

    x_block = lax.all_gather(
        x_piece.astype(jnp.float16), ("xh", "xl", "core"), axis=0, tiled=True
    ).astype(BF16)

    partial_panel = lax.dot_general(
        x_rows, x_block, (((1,), (0,)), ((), ())), preferred_element_type=F32
    )
    quarter = half // 4
    parts = partial_panel.reshape(4, quarter, BLK)
    message = quantize(parts)
    total = lax.dynamic_index_in_dim(parts, y, 0, False)
    for shift in (1, 3, 2):
        sent = lax.dynamic_index_in_dim(message, (y + shift) % 4, 0, False)
        total = total + dequantize(ring("y", 4, shift, sent))
    panel = lax.all_gather(quantize(total), ("y", "core"), axis=0)
    panel = panel.reshape(4, 2, quarter + 16, BLK)
    scales = scales_of(panel) * (2.0 / token_total)

    chosen = (scale_index[:, :, None] == jnp.arange(LEVELS, dtype=jnp.int32)).astype(F32)
    group_scale = jnp.sum(chosen * scale_table, axis=2)
    quantized = jnp.repeat(group_scale, GROUP, axis=0) * (codes.astype(F32) - 7.5)

    wide = w_piece.shape[1]
    own_columns = lax.dynamic_slice_in_dim(quantized, x * wide, wide, 1)
    error = quantize_columns(block_error(inverse, w_piece, own_columns))
    errors = [error]
    for shift in (1, 2, 3):
        errors.append(lax.ppermute(error, PLANE, plane_pairs(range(4), shift)))

    first_local = block_index[0] * BLK - tile * shard_rows
    padded = jnp.pad(quantized.astype(BF16), [(shard_rows, shard_rows), (0, 0)])
    begin = jnp.clip(shard_rows - first_local, 0, BLK + shard_rows)
    quant_rows = lax.dynamic_slice_in_dim(padded, begin, shard_rows, 0)
    row = jnp.arange(shard_rows, dtype=jnp.int32)[:, None] - first_local
    base = jnp.where((row >= 0) & (row < BLK), quant_rows, weights)
    scalars = jnp.stack([first_local + BLK, x])
    return apply_update(scalars, panel, scales, errors, base)


def solution(mesh):
    cube = Mesh(mesh.devices.reshape(4, 2, 2, 8, 2), ("y", "core") + PLANE)
    return jax.shard_map(
        local,
        mesh=cube,
        in_specs=(
            P(("y", "core"), PLANE),
            P(PLANE, ("y", "core")),
            P(None, ("y", "core")),
            P(None, ("y", "core")),
            P(),
            P(PLANE, None),
            P(),
        ),
        out_specs=P(PLANE, ("y", "core")),
        check_vma=False,
    )
```

```python
import functools
import jax
import jax.numpy as jnp
from jax import lax
from jax.experimental import pallas as pl
from jax.experimental.pallas import tpu as pltpu
from jax.sharding import Mesh, PartitionSpec as P

BLK = 1024
GROUP = 128
LEVELS = 16
UNIT = 128
UNITS = BLK // UNIT
STEPS_PER_OCTAVE = 128.0
F32, BF16, S16 = jnp.float32, jnp.bfloat16, jnp.int16
PLANE = ("xl", "z", "xh")


def tile_at(x, z):
    return (x % 2) * 16 + (z % 8) * 2 + (x % 4) // 2


def ring(axis, size, shift, value):
    return lax.ppermute(value, axis, [(i, (i + shift) % size) for i in range(size)])


def pick_kernel(rows, cols, scalars, src_ref, *out_refs):
    x = scalars[UNITS]
    for k, out_ref in enumerate(out_refs):
        p = (x + k) % 4
        if rows is not None:
            out_ref[...] = src_ref[pl.ds(pl.multiple_of(p * rows, rows), rows), :]
        else:
            out_ref[...] = src_ref[:, pl.ds(pl.multiple_of(p * cols, cols), cols)]


def pick(source, along, scalars, name):
    other = source.shape[1 - along]
    part = other // 4
    if along == 1:
        in_spec = pl.BlockSpec((other, UNIT), lambda j, u: (0, u[j]))
        out_spec = pl.BlockSpec((part, UNIT), lambda j, u: (0, j))
        shape, rows, cols = (part, BLK), part, None
    else:
        in_spec = pl.BlockSpec((UNIT, other), lambda j, u: (u[j], 0))
        out_spec = pl.BlockSpec((UNIT, part), lambda j, u: (j, 0))
        shape, rows, cols = (BLK, part), None, part
    return pl.pallas_call(
        functools.partial(pick_kernel, rows, cols),
        grid_spec=pltpu.PrefetchScalarGridSpec(
            num_scalar_prefetch=1, grid=(UNITS,), in_specs=[in_spec], out_specs=[out_spec] * 4
        ),
        out_shape=[jax.ShapeDtypeStruct(shape, BF16)] * 4,
        name=name,
    )(scalars, source)


def plane_pairs(columns, shift):
    return [(tile_at(s, z), tile_at(s + shift, z)) for s in columns for z in range(8)]


def scatter_x(pieces, x, from_low):
    own, *others = pieces
    up, across, down = (
        lax.ppermute(piece, PLANE, plane_pairs((0, 2), shift))
        for shift, piece in zip((1, 2, 3), others)
    )
    even = x % 2 == 0
    near = jnp.where(even, own, up)
    far = jnp.where(even, across, down)
    return jnp.where(from_low, near, far)


def reach_far(piece, distance, beside=()):
    up, down = ring("z", 8, 3, piece), ring("z", 8, -3, piece)
    up, down, *beside = lax.optimization_barrier((up, down, *beside))
    return jnp.where(distance == 3, up, jnp.where(distance == 5, down, piece)), *beside


def reach_near(piece, distance):
    up, down = ring("z", 8, 1, piece), ring("z", 8, -1, piece)
    from_below = (distance == 1) | (distance == 4) | (distance == 6)
    from_above = (distance == 7) | (distance == 2)
    return jnp.where(from_below, up, jnp.where(from_above, down, piece))


def quantize(values):
    rows = values.shape[-2]
    top = jnp.max(jnp.abs(values), axis=-1, keepdims=True)
    level = jnp.floor(jnp.log2(32700.0 / jnp.maximum(top, 1e-25)) * STEPS_PER_OCTAVE)
    scaled = jnp.round(values * jnp.exp2(level / STEPS_PER_OCTAVE)).astype(jnp.int32).astype(S16)
    levels = jnp.swapaxes(level, -1, -2).astype(jnp.int32).astype(S16)
    widths = [(0, 0)] * (values.ndim - 2) + [(0, 15), (0, values.shape[-1] - rows)]
    return jnp.concatenate([scaled, jnp.pad(levels, widths)], axis=-2)


def scales_of(message):
    rows = message.shape[-2] - 16
    level = message[..., rows : rows + 1, :rows].astype(F32)
    return jnp.swapaxes(jnp.exp2(-level / STEPS_PER_OCTAVE), -1, -2)


def dequantize(message):
    return message[..., :-16, :].astype(F32) * scales_of(message)


def split(values):
    high = values.astype(BF16)
    return high, (values - high.astype(F32)).astype(BF16)


def mm(a, b):
    return jnp.dot(a, b, preferred_element_type=F32)


def error_kernel(inv_ref, w_ref, q_ref, out_ref):
    inv_high, inv_low = split(inv_ref[...])
    dev_high, dev_low = split(w_ref[...].astype(F32) - q_ref[...])
    error = mm(inv_high, dev_high) + (mm(inv_high, dev_low) + mm(inv_low, dev_high))
    i = pl.program_id(0)
    first = ((i % 2) * 16 + i // 2) * 32
    for z in range(8):
        at = pl.multiple_of(first + z * 64, 32)
        out_ref[pl.ds(at, 32), :] = error[z * 32 : (z + 1) * 32]


def block_error(inverse, w_piece, quantized):
    wide = w_piece.shape[1]
    whole = pl.BlockSpec((BLK, wide), lambda i: (0, 0))
    return pl.pallas_call(
        error_kernel,
        grid=(4,),
        in_specs=[pl.BlockSpec((BLK // 4, BLK), lambda i: (i, 0)), whole, whole],
        out_specs=whole,
        out_shape=jax.ShapeDtypeStruct((BLK, wide), F32),
        compiler_params=pltpu.CompilerParams(vmem_limit_bytes=32 << 20),
        cost_estimate=pl.CostEstimate(
            flops=6 * BLK * BLK * wide, bytes_accessed=BLK * BLK * 4, transcendentals=0
        ),
        name="block_error",
    )(inverse, w_piece, quantized)


def quantize_columns(error):
    top = jnp.max(jnp.abs(error), axis=0, keepdims=True)
    level = jnp.floor(jnp.log2(32700.0 / jnp.maximum(top, 1e-25)) * STEPS_PER_OCTAVE)
    scaled = jnp.round(error * jnp.exp2(level / STEPS_PER_OCTAVE))
    levels = jnp.broadcast_to(level, (16, error.shape[1]))
    return jnp.concatenate([scaled, levels], axis=0).astype(jnp.int32).astype(S16)


def update_kernel(scalars, h_ref, scale_ref, e0, e1, e2, e3, base_ref, out_ref, high_ref, low_ref, factor_ref):
    rows, wide = out_ref.shape[0], e0.shape[1]

    @pl.when(pl.program_id(0) == 0)
    def _():
        for k, e in enumerate((e0, e1, e2, e3)):
            high_ref[k], low_ref[k] = split(e[:BLK].astype(jnp.int32).astype(F32))
            level = e[BLK : BLK + 16].astype(jnp.int32).astype(F32)
            factor_ref[k] = jnp.exp2(level * (-1.0 / STEPS_PER_OCTAVE))

    h_high, h_low = split(h_ref[0, 0, :rows].astype(jnp.int32).astype(F32))
    row = lax.broadcasted_iota(jnp.int32, (rows, wide), 0) + pl.program_id(0) * rows
    for k in range(4):
        cols = pl.ds(pl.multiple_of(((scalars[1] + 4 - k) % 4) * wide, wide), wide)
        update = mm(h_high, high_ref[k]) + (mm(h_high, low_ref[k]) + mm(h_low, high_ref[k]))
        update = update * scale_ref[0, 0] * factor_ref[k, 0:1]
        base = base_ref[:, cols].astype(F32)
        out_ref[:, cols] = jnp.where(row >= scalars[0], base - update, base).astype(BF16)


def apply_update(scalars, panel, scales, errors, base):
    rows, cols = panel.shape[2] - 16, base.shape[1]
    wide = cols // 4
    whole = pl.BlockSpec((BLK + 16, wide), lambda i, s: (0, 0))
    stripe = pl.BlockSpec((rows, cols), lambda i, s: (i, 0))
    return pl.pallas_call(
        update_kernel,
        grid_spec=pltpu.PrefetchScalarGridSpec(
            num_scalar_prefetch=1,
            grid=(base.shape[0] // rows,),
            in_specs=[
                pl.BlockSpec((1, 1, rows + 16, BLK), lambda i, s: (i % 4, i // 4, 0, 0)),
                pl.BlockSpec((1, 1, rows, 1), lambda i, s: (i % 4, i // 4, 0, 0)),
                whole,
                whole,
                whole,
                whole,
                stripe,
            ],
            out_specs=stripe,
            scratch_shapes=[
                pltpu.VMEM((4, BLK, wide), BF16),
                pltpu.VMEM((4, BLK, wide), BF16),
                pltpu.VMEM((4, 16, wide), F32),
            ],
        ),
        out_shape=jax.ShapeDtypeStruct(base.shape, BF16),
        compiler_params=pltpu.CompilerParams(vmem_limit_bytes=32 << 20),
        cost_estimate=pl.CostEstimate(
            flops=6 * base.shape[0] * BLK * cols,
            bytes_accessed=base.shape[0] * cols * 6 + BLK * cols * 2,
            transcendentals=0,
        ),
        name="apply_update",
    )(scalars, panel, scales, *errors, base)


def local(activations, weights, codes, scale_index, scale_table, inverse_block, block_index):
    y, core = lax.axis_index("y"), lax.axis_index("core")
    xl, z, xh = (lax.axis_index(a) for a in PLANE)
    x = 2 * xh + xl
    tile = lax.axis_index(PLANE)
    shard_rows = weights.shape[0]
    tile_units = shard_rows // UNIT
    token_total = activations.shape[0] * 8
    first_unit = block_index[0] * UNITS
    units = first_unit + jnp.arange(UNITS, dtype=jnp.int32)
    owner = units // tile_units
    x_owner, z_owner = 2 * (owner % 2), (owner // 2) % 8
    distance = (z - z_owner) % 8
    from_low = x_owner == jnp.where(x % 2 == 0, x, (x + 3) % 4)

    own_rows = inverse_block.shape[0] // 2
    inverse_part = lax.dynamic_slice_in_dim(inverse_block, core * own_rows, own_rows, 0)
    inverse_part, activations = lax.optimization_barrier((inverse_part, activations))
    inverse = lax.all_gather(inverse_part, ("xh", "xl", "z", "core"), axis=0)
    inverse = inverse.reshape(BLK, BLK)

    index = jnp.clip(units - tile * tile_units, 0, tile_units - 1)
    picks = jnp.append(index, x)
    x_pieces = pick(activations, 1, picks, "pick_columns")
    w_pieces = pick(weights, 0, picks, "pick_rows")

    half = shard_rows // 2
    x_mine = lax.dynamic_slice_in_dim(activations, core * half, half, 1)
    x_theirs = lax.dynamic_slice_in_dim(activations, (1 - core) * half, half, 1)
    x_other = ring("core", 2, 1, x_theirs)
    x_low = jnp.where(core == 0, x_mine, x_other)
    x_high = jnp.where(core == 0, x_other, x_mine)
    x_rows = jnp.concatenate(
        [v[128 * p : 128 * (p + 1)] for p in range(4) for v in (x_low, x_high)], axis=0
    ).T

    lanes = lambda v: jnp.repeat(v, UNIT)[None, :]
    sublanes = lambda v: jnp.repeat(v, UNIT)[:, None]
    x_piece = scatter_x(x_pieces, x, lanes(from_low))
    x_piece, w_pieces = lax.optimization_barrier((x_piece, w_pieces))
    w_piece = scatter_x(w_pieces, x, sublanes(from_low))
    x_piece, x_rows = reach_far(x_piece, lanes(distance), (x_rows,))
    x_piece, w_piece = lax.optimization_barrier((x_piece, w_piece))
    x_piece = reach_near(x_piece, lanes(distance))

    x_block = lax.all_gather(
        x_piece.astype(jnp.float16), ("xh", "xl", "core"), axis=0, tiled=True
    ).astype(BF16)

    partial_panel = lax.dot_general(
        x_rows, x_block, (((1,), (0,)), ((), ())), preferred_element_type=F32
    )
    w_piece, partial_panel = reach_far(w_piece, sublanes(distance), (partial_panel,))
    w_piece = reach_near(w_piece, sublanes(distance))
    quarter = half // 4
    parts = partial_panel.reshape(4, quarter, BLK)
    message = quantize(parts)
    message, codes, scale_index = lax.optimization_barrier((message, codes, scale_index))
    total = lax.dynamic_index_in_dim(parts, y, 0, False)
    for shift in (1, 3, 2):
        sent = lax.dynamic_index_in_dim(message, (y + shift) % 4, 0, False)
        total = total + dequantize(ring("y", 4, shift, sent))
    chosen = (scale_index[:, :, None] == jnp.arange(LEVELS, dtype=jnp.int32)).astype(F32)
    group_scale = jnp.sum(chosen * scale_table, axis=2)
    quantized = jnp.repeat(group_scale, GROUP, axis=0) * (codes.astype(F32) - 7.5)

    wide = w_piece.shape[1]
    own_columns = lax.dynamic_slice_in_dim(quantized, x * wide, wide, 1)
    error = quantize_columns(block_error(inverse, w_piece, own_columns))
    total, error = lax.optimization_barrier((total, error))
    panel = lax.all_gather(quantize(total), ("y", "core"), axis=0)
    panel = panel.reshape(4, 2, quarter + 16, BLK)
    scales = scales_of(panel) * (2.0 / token_total)

    errors = [error]
    for shift in (1, 2, 3):
        errors.append(lax.ppermute(error, PLANE, plane_pairs(range(4), shift)))

    first_local = block_index[0] * BLK - tile * shard_rows
    padded = jnp.pad(quantized.astype(BF16), [(shard_rows, shard_rows), (0, 0)])
    begin = jnp.clip(shard_rows - first_local, 0, BLK + shard_rows)
    quant_rows = lax.dynamic_slice_in_dim(padded, begin, shard_rows, 0)
    row = jnp.arange(shard_rows, dtype=jnp.int32)[:, None] - first_local
    base = jnp.where((row >= 0) & (row < BLK), quant_rows, weights)
    scalars = jnp.stack([first_local + BLK, x])
    return apply_update(scalars, panel, scales, errors, base)


def solution(mesh):
    cube = Mesh(mesh.devices.reshape(4, 2, 2, 8, 2), ("y", "core") + PLANE)
    return jax.shard_map(
        local,
        mesh=cube,
        in_specs=(
            P(("y", "core"), PLANE),
            P(PLANE, ("y", "core")),
            P(None, ("y", "core")),
            P(None, ("y", "core")),
            P(),
            P(PLANE, None),
            P(),
        ),
        out_specs=P(PLANE, ("y", "core")),
        check_vma=False,
    )
```

```python
import functools
import jax
import jax.numpy as jnp
from jax import lax
from jax.experimental import pallas as pl
from jax.experimental.pallas import tpu as pltpu
from jax.sharding import Mesh, PartitionSpec as P

BLK = 1024
GROUP = 128
LEVELS = 16
UNIT = 128
UNITS = BLK // UNIT
STEPS_PER_OCTAVE = 128.0
F32, BF16, S16 = jnp.float32, jnp.bfloat16, jnp.int16
PLANE = ("xl", "z", "xh")


def tile_at(x, z):
    return (x % 2) * 16 + (z % 8) * 2 + (x % 4) // 2


def ring(axis, size, shift, value):
    return lax.ppermute(value, axis, [(i, (i + shift) % size) for i in range(size)])


def pick_kernel(rows, cols, scalars, src_ref, *out_refs):
    x = scalars[UNITS]
    for k, out_ref in enumerate(out_refs):
        p = (x + k) % 4
        if rows is not None:
            out_ref[...] = src_ref[pl.ds(pl.multiple_of(p * rows, rows), rows), :]
        else:
            out_ref[...] = src_ref[:, pl.ds(pl.multiple_of(p * cols, cols), cols)]


def pick(source, along, scalars, name):
    other = source.shape[1 - along]
    part = other // 4
    if along == 1:
        in_spec = pl.BlockSpec((other, UNIT), lambda j, u: (0, u[j]))
        out_spec = pl.BlockSpec((part, UNIT), lambda j, u: (0, j))
        shape, rows, cols = (part, BLK), part, None
    else:
        in_spec = pl.BlockSpec((UNIT, other), lambda j, u: (u[j], 0))
        out_spec = pl.BlockSpec((UNIT, part), lambda j, u: (j, 0))
        shape, rows, cols = (BLK, part), None, part
    return pl.pallas_call(
        functools.partial(pick_kernel, rows, cols),
        grid_spec=pltpu.PrefetchScalarGridSpec(
            num_scalar_prefetch=1, grid=(UNITS,), in_specs=[in_spec], out_specs=[out_spec] * 4
        ),
        out_shape=[jax.ShapeDtypeStruct(shape, BF16)] * 4,
        name=name,
    )(scalars, source)


def plane_pairs(columns, shift):
    return [(tile_at(s, z), tile_at(s + shift, z)) for s in columns for z in range(8)]


def scatter_x(pieces, x, from_low):
    own, *others = pieces
    up, across, down = (
        lax.ppermute(piece, PLANE, plane_pairs((0, 2), shift))
        for shift, piece in zip((1, 2, 3), others)
    )
    even = x % 2 == 0
    near = jnp.where(even, own, up)
    far = jnp.where(even, across, down)
    return jnp.where(from_low, near, far)


def reach_far(piece, distance, beside=()):
    up, down = ring("z", 8, 3, piece), ring("z", 8, -3, piece)
    up, down, *beside = lax.optimization_barrier((up, down, *beside))
    return jnp.where(distance == 3, up, jnp.where(distance == 5, down, piece)), *beside


def reach_near(piece, distance):
    up, down = ring("z", 8, 1, piece), ring("z", 8, -1, piece)
    from_below = (distance == 1) | (distance == 4) | (distance == 6)
    from_above = (distance == 7) | (distance == 2)
    return jnp.where(from_below, up, jnp.where(from_above, down, piece))


def spread_from(z0, piece, z, z_owner):
    at = lambda d: (z0 + d) % 8
    send = lambda value, pairs: lax.ppermute(value, "z", [(at(a), at(b)) for a, b in pairs])
    place = (z - z0) % 8
    got = send(piece, [(0, 1), (1, 0)])
    piece = jnp.where((place <= 1) & (z_owner != z), got, piece)
    got = send(piece, [(0, 6), (1, 3)])
    piece = jnp.where((place == 6) | (place == 3), got, piece)
    got = send(piece, [(0, 7), (1, 2), (6, 5), (3, 4)])
    odd = (place == 7) | (place == 2) | (place == 5) | (place == 4)
    return jnp.where(odd, got, piece)


def quantize(values):
    rows = values.shape[-2]
    top = jnp.max(jnp.abs(values), axis=-1, keepdims=True)
    level = jnp.floor(jnp.log2(32700.0 / jnp.maximum(top, 1e-25)) * STEPS_PER_OCTAVE)
    scaled = jnp.round(values * jnp.exp2(level / STEPS_PER_OCTAVE)).astype(jnp.int32).astype(S16)
    levels = jnp.swapaxes(level, -1, -2).astype(jnp.int32).astype(S16)
    widths = [(0, 0)] * (values.ndim - 2) + [(0, 15), (0, values.shape[-1] - rows)]
    return jnp.concatenate([scaled, jnp.pad(levels, widths)], axis=-2)


def scales_of(message):
    rows = message.shape[-2] - 16
    level = message[..., rows : rows + 1, :rows].astype(F32)
    return jnp.swapaxes(jnp.exp2(-level / STEPS_PER_OCTAVE), -1, -2)


def dequantize(message):
    return message[..., :-16, :].astype(F32) * scales_of(message)


def split(values):
    high = values.astype(BF16)
    return high, (values - high.astype(F32)).astype(BF16)


def mm(a, b):
    return jnp.dot(a, b, preferred_element_type=F32)


def error_kernel(inv_ref, w_ref, q_ref, out_ref):
    inv_high, inv_low = split(inv_ref[...])
    dev_high, dev_low = split(w_ref[...].astype(F32) - q_ref[...])
    error = mm(inv_high, dev_high) + (mm(inv_high, dev_low) + mm(inv_low, dev_high))
    i = pl.program_id(0)
    first = ((i % 2) * 16 + i // 2) * 32
    for z in range(8):
        at = pl.multiple_of(first + z * 64, 32)
        out_ref[pl.ds(at, 32), :] = error[z * 32 : (z + 1) * 32]


def block_error(inverse, w_piece, quantized):
    wide = w_piece.shape[1]
    whole = pl.BlockSpec((BLK, wide), lambda i: (0, 0))
    return pl.pallas_call(
        error_kernel,
        grid=(4,),
        in_specs=[pl.BlockSpec((BLK // 4, BLK), lambda i: (i, 0)), whole, whole],
        out_specs=whole,
        out_shape=jax.ShapeDtypeStruct((BLK, wide), F32),
        compiler_params=pltpu.CompilerParams(vmem_limit_bytes=32 << 20),
        cost_estimate=pl.CostEstimate(
            flops=6 * BLK * BLK * wide, bytes_accessed=BLK * BLK * 4, transcendentals=0
        ),
        name="block_error",
    )(inverse, w_piece, quantized)


def quantize_columns(error):
    top = jnp.max(jnp.abs(error), axis=0, keepdims=True)
    level = jnp.floor(jnp.log2(32700.0 / jnp.maximum(top, 1e-25)) * STEPS_PER_OCTAVE)
    scaled = jnp.round(error * jnp.exp2(level / STEPS_PER_OCTAVE))
    levels = jnp.broadcast_to(level, (16, error.shape[1]))
    return jnp.concatenate([scaled, levels], axis=0).astype(jnp.int32).astype(S16)


def update_kernel(scalars, h_ref, scale_ref, e0, e1, e2, e3, base_ref, out_ref, high_ref, low_ref, factor_ref):
    rows, wide = out_ref.shape[0], e0.shape[1]

    @pl.when(pl.program_id(0) == 0)
    def _():
        for k, e in enumerate((e0, e1, e2, e3)):
            high_ref[k], low_ref[k] = split(e[:BLK].astype(jnp.int32).astype(F32))
            level = e[BLK : BLK + 16].astype(jnp.int32).astype(F32)
            factor_ref[k] = jnp.exp2(level * (-1.0 / STEPS_PER_OCTAVE))

    h_high, h_low = split(h_ref[0, 0, :rows].astype(jnp.int32).astype(F32))
    row = lax.broadcasted_iota(jnp.int32, (rows, wide), 0) + pl.program_id(0) * rows
    for k in range(4):
        cols = pl.ds(pl.multiple_of(((scalars[1] + 4 - k) % 4) * wide, wide), wide)
        update = mm(h_high, high_ref[k]) + (mm(h_high, low_ref[k]) + mm(h_low, high_ref[k]))
        update = update * scale_ref[0, 0] * factor_ref[k, 0:1]
        base = base_ref[:, cols].astype(F32)
        out_ref[:, cols] = jnp.where(row >= scalars[0], base - update, base).astype(BF16)


def apply_update(scalars, panel, scales, errors, base):
    rows, cols = panel.shape[2] - 16, base.shape[1]
    wide = cols // 4
    whole = pl.BlockSpec((BLK + 16, wide), lambda i, s: (0, 0))
    stripe = pl.BlockSpec((rows, cols), lambda i, s: (i, 0))
    return pl.pallas_call(
        update_kernel,
        grid_spec=pltpu.PrefetchScalarGridSpec(
            num_scalar_prefetch=1,
            grid=(base.shape[0] // rows,),
            in_specs=[
                pl.BlockSpec((1, 1, rows + 16, BLK), lambda i, s: (i % 4, i // 4, 0, 0)),
                pl.BlockSpec((1, 1, rows, 1), lambda i, s: (i % 4, i // 4, 0, 0)),
                whole,
                whole,
                whole,
                whole,
                stripe,
            ],
            out_specs=stripe,
            scratch_shapes=[
                pltpu.VMEM((4, BLK, wide), BF16),
                pltpu.VMEM((4, BLK, wide), BF16),
                pltpu.VMEM((4, 16, wide), F32),
            ],
        ),
        out_shape=jax.ShapeDtypeStruct(base.shape, BF16),
        compiler_params=pltpu.CompilerParams(vmem_limit_bytes=32 << 20),
        cost_estimate=pl.CostEstimate(
            flops=6 * base.shape[0] * BLK * cols,
            bytes_accessed=base.shape[0] * cols * 6 + BLK * cols * 2,
            transcendentals=0,
        ),
        name="apply_update",
    )(scalars, panel, scales, *errors, base)


def local(activations, weights, codes, scale_index, scale_table, inverse_block, block_index):
    y, core = lax.axis_index("y"), lax.axis_index("core")
    xl, z, xh = (lax.axis_index(a) for a in PLANE)
    x = 2 * xh + xl
    tile = lax.axis_index(PLANE)
    shard_rows = weights.shape[0]
    tile_units = shard_rows // UNIT
    token_total = activations.shape[0] * 8
    first_unit = block_index[0] * UNITS
    units = first_unit + jnp.arange(UNITS, dtype=jnp.int32)
    owner = units // tile_units
    x_owner, z_owner = 2 * (owner % 2), (owner // 2) % 8
    distance = (z - z_owner) % 8
    from_low = x_owner == jnp.where(x % 2 == 0, x, (x + 3) % 4)

    own_rows = inverse_block.shape[0] // 2
    inverse_part = lax.dynamic_slice_in_dim(inverse_block, core * own_rows, own_rows, 0)
    inverse_part, activations = lax.optimization_barrier((inverse_part, activations))
    inverse = lax.all_gather(inverse_part, ("xh", "xl", "z", "core"), axis=0)
    inverse = inverse.reshape(BLK, BLK)

    index = jnp.clip(units - tile * tile_units, 0, tile_units - 1)
    picks = jnp.append(index, x)
    x_pieces = pick(activations, 1, picks, "pick_columns")
    w_pieces = pick(weights, 0, picks, "pick_rows")

    half = shard_rows // 2
    x_mine = lax.dynamic_slice_in_dim(activations, core * half, half, 1)
    x_theirs = lax.dynamic_slice_in_dim(activations, (1 - core) * half, half, 1)
    x_other = ring("core", 2, 1, x_theirs)
    x_low = jnp.where(core == 0, x_mine, x_other)
    x_high = jnp.where(core == 0, x_other, x_mine)
    x_rows = jnp.concatenate(
        [v[128 * p : 128 * (p + 1)] for p in range(4) for v in (x_low, x_high)], axis=0
    ).T

    lanes = lambda v: jnp.repeat(v, UNIT)[None, :]
    sublanes = lambda v: jnp.repeat(v, UNIT)[:, None]
    x_piece = scatter_x(x_pieces, x, lanes(from_low))
    w_piece = scatter_x(w_pieces, x, sublanes(from_low))
    x_piece = lax.switch(
        (first_unit // tile_units // 2) % 8,
        [functools.partial(spread_from, z0) for z0 in range(8)],
        x_piece,
        z,
        lanes(z_owner),
    )
    x_piece, w_piece, x_rows = lax.optimization_barrier((x_piece, w_piece, x_rows))

    x_block = lax.all_gather(
        x_piece.astype(jnp.float16), ("xh", "xl", "core"), axis=0, tiled=True
    ).astype(BF16)

    partial_panel = lax.dot_general(
        x_rows, x_block, (((1,), (0,)), ((), ())), preferred_element_type=F32
    )
    w_piece, partial_panel = reach_far(w_piece, sublanes(distance), (partial_panel,))
    w_piece = reach_near(w_piece, sublanes(distance))
    quarter = half // 4
    parts = partial_panel.reshape(4, quarter, BLK)
    message = quantize(parts)
    message, codes, scale_index = lax.optimization_barrier((message, codes, scale_index))
    total = lax.dynamic_index_in_dim(parts, y, 0, False)
    for shift in (1, 3, 2):
        sent = lax.dynamic_index_in_dim(message, (y + shift) % 4, 0, False)
        total = total + dequantize(ring("y", 4, shift, sent))
    chosen = (scale_index[:, :, None] == jnp.arange(LEVELS, dtype=jnp.int32)).astype(F32)
    group_scale = jnp.sum(chosen * scale_table, axis=2)
    quantized = jnp.repeat(group_scale, GROUP, axis=0) * (codes.astype(F32) - 7.5)

    wide = w_piece.shape[1]
    own_columns = lax.dynamic_slice_in_dim(quantized, x * wide, wide, 1)
    error = quantize_columns(block_error(inverse, w_piece, own_columns))
    total, error = lax.optimization_barrier((total, error))
    panel = lax.all_gather(quantize(total), ("y", "core"), axis=0)
    panel = panel.reshape(4, 2, quarter + 16, BLK)
    scales = scales_of(panel) * (2.0 / token_total)

    errors = [error]
    for shift in (1, 2, 3):
        errors.append(lax.ppermute(error, PLANE, plane_pairs(range(4), shift)))

    first_local = block_index[0] * BLK - tile * shard_rows
    padded = jnp.pad(quantized.astype(BF16), [(shard_rows, shard_rows), (0, 0)])
    begin = jnp.clip(shard_rows - first_local, 0, BLK + shard_rows)
    quant_rows = lax.dynamic_slice_in_dim(padded, begin, shard_rows, 0)
    row = jnp.arange(shard_rows, dtype=jnp.int32)[:, None] - first_local
    base = jnp.where((row >= 0) & (row < BLK), quant_rows, weights)
    scalars = jnp.stack([first_local + BLK, x])
    return apply_update(scalars, panel, scales, errors, base)


def solution(mesh):
    cube = Mesh(mesh.devices.reshape(4, 2, 2, 8, 2), ("y", "core") + PLANE)
    return jax.shard_map(
        local,
        mesh=cube,
        in_specs=(
            P(("y", "core"), PLANE),
            P(PLANE, ("y", "core")),
            P(None, ("y", "core")),
            P(None, ("y", "core")),
            P(),
            P(PLANE, None),
            P(),
        ),
        out_specs=P(PLANE, ("y", "core")),
        check_vma=False,
    )
```

```python
import functools
import jax
import jax.numpy as jnp
from jax import lax
from jax.experimental import pallas as pl
from jax.experimental.pallas import tpu as pltpu
from jax.sharding import Mesh, PartitionSpec as P

BLK = 1024
GROUP = 128
LEVELS = 16
UNIT = 128
UNITS = BLK // UNIT
STEPS_PER_OCTAVE = 128.0
F32, BF16, S16 = jnp.float32, jnp.bfloat16, jnp.int16
PLANE = ("xl", "z", "xh")


def tile_at(x, z):
    return (x % 2) * 16 + (z % 8) * 2 + (x % 4) // 2


def ring(axis, size, shift, value):
    return lax.ppermute(value, axis, [(i, (i + shift) % size) for i in range(size)])


def pick_kernel(rows, cols, scalars, src_ref, *out_refs):
    x = scalars[UNITS]
    for k, out_ref in enumerate(out_refs):
        p = (x + k) % 4
        if rows is not None:
            out_ref[...] = src_ref[pl.ds(pl.multiple_of(p * rows, rows), rows), :]
        else:
            out_ref[...] = src_ref[:, pl.ds(pl.multiple_of(p * cols, cols), cols)]


def pick(source, along, scalars, name):
    other = source.shape[1 - along]
    part = other // 4
    if along == 1:
        in_spec = pl.BlockSpec((other, UNIT), lambda j, u: (0, u[j]))
        out_spec = pl.BlockSpec((part, UNIT), lambda j, u: (0, j))
        shape, rows, cols = (part, BLK), part, None
    else:
        in_spec = pl.BlockSpec((UNIT, other), lambda j, u: (u[j], 0))
        out_spec = pl.BlockSpec((UNIT, part), lambda j, u: (j, 0))
        shape, rows, cols = (BLK, part), None, part
    return pl.pallas_call(
        functools.partial(pick_kernel, rows, cols),
        grid_spec=pltpu.PrefetchScalarGridSpec(
            num_scalar_prefetch=1, grid=(UNITS,), in_specs=[in_spec], out_specs=[out_spec] * 4
        ),
        out_shape=[jax.ShapeDtypeStruct(shape, BF16)] * 4,
        name=name,
    )(scalars, source)


def plane_pairs(columns, shift):
    return [(tile_at(s, z), tile_at(s + shift, z)) for s in columns for z in range(8)]


def scatter_x(pieces, x, from_low):
    own, *others = pieces
    up, across, down = (
        lax.ppermute(piece, PLANE, plane_pairs((0, 2), shift))
        for shift, piece in zip((1, 2, 3), others)
    )
    even = x % 2 == 0
    near = jnp.where(even, own, up)
    far = jnp.where(even, across, down)
    return jnp.where(from_low, near, far)


def reach_far(piece, distance, beside=()):
    up, down = ring("z", 8, 3, piece), ring("z", 8, -3, piece)
    up, down, *beside = lax.optimization_barrier((up, down, *beside))
    return jnp.where(distance == 3, up, jnp.where(distance == 5, down, piece)), *beside


def reach_near(piece, distance):
    up, down = ring("z", 8, 1, piece), ring("z", 8, -1, piece)
    from_below = (distance == 1) | (distance == 4) | (distance == 6)
    from_above = (distance == 7) | (distance == 2)
    return jnp.where(from_below, up, jnp.where(from_above, down, piece))


def quantize(values):
    rows = values.shape[-2]
    top = jnp.max(jnp.abs(values), axis=-1, keepdims=True)
    level = jnp.floor(jnp.log2(32700.0 / jnp.maximum(top, 1e-25)) * STEPS_PER_OCTAVE)
    scaled = jnp.round(values * jnp.exp2(level / STEPS_PER_OCTAVE)).astype(jnp.int32).astype(S16)
    levels = jnp.swapaxes(level, -1, -2).astype(jnp.int32).astype(S16)
    widths = [(0, 0)] * (values.ndim - 2) + [(0, 15), (0, values.shape[-1] - rows)]
    return jnp.concatenate([scaled, jnp.pad(levels, widths)], axis=-2)


def scales_of(message):
    rows = message.shape[-2] - 16
    level = message[..., rows : rows + 1, :rows].astype(F32)
    return jnp.swapaxes(jnp.exp2(-level / STEPS_PER_OCTAVE), -1, -2)


def dequantize(message):
    return message[..., :-16, :].astype(F32) * scales_of(message)


def split(values):
    high = values.astype(BF16)
    return high, (values - high.astype(F32)).astype(BF16)


def mm(a, b):
    return jnp.dot(a, b, preferred_element_type=F32)


def error_kernel(inv_ref, w_ref, q_ref, out_ref):
    inv_high, inv_low = split(inv_ref[...])
    dev_high, dev_low = split(w_ref[...].astype(F32) - q_ref[...])
    error = mm(inv_high, dev_high) + (mm(inv_high, dev_low) + mm(inv_low, dev_high))
    i = pl.program_id(0)
    first = ((i % 2) * 16 + i // 2) * 32
    for z in range(8):
        at = pl.multiple_of(first + z * 64, 32)
        out_ref[pl.ds(at, 32), :] = error[z * 32 : (z + 1) * 32]


def block_error(inverse, w_piece, quantized):
    wide = w_piece.shape[1]
    whole = pl.BlockSpec((BLK, wide), lambda i: (0, 0))
    return pl.pallas_call(
        error_kernel,
        grid=(4,),
        in_specs=[pl.BlockSpec((BLK // 4, BLK), lambda i: (i, 0)), whole, whole],
        out_specs=whole,
        out_shape=jax.ShapeDtypeStruct((BLK, wide), F32),
        compiler_params=pltpu.CompilerParams(vmem_limit_bytes=32 << 20),
        cost_estimate=pl.CostEstimate(
            flops=6 * BLK * BLK * wide, bytes_accessed=BLK * BLK * 4, transcendentals=0
        ),
        name="block_error",
    )(inverse, w_piece, quantized)


def quantize_columns(error):
    top = jnp.max(jnp.abs(error), axis=0, keepdims=True)
    level = jnp.floor(jnp.log2(32700.0 / jnp.maximum(top, 1e-25)) * STEPS_PER_OCTAVE)
    scaled = jnp.round(error * jnp.exp2(level / STEPS_PER_OCTAVE))
    levels = jnp.broadcast_to(level, (16, error.shape[1]))
    return jnp.concatenate([scaled, levels], axis=0).astype(jnp.int32).astype(S16)


def update_kernel(scalars, h_ref, scale_ref, e0, e1, e2, e3, base_ref, out_ref, high_ref, low_ref, factor_ref):
    rows, wide = out_ref.shape[0], e0.shape[1]

    @pl.when(pl.program_id(0) == 0)
    def _():
        for k, e in enumerate((e0, e1, e2, e3)):
            high_ref[k], low_ref[k] = split(e[:BLK].astype(jnp.int32).astype(F32))
            level = e[BLK : BLK + 16].astype(jnp.int32).astype(F32)
            factor_ref[k] = jnp.exp2(level * (-1.0 / STEPS_PER_OCTAVE))

    part = rows // 2
    h = jnp.concatenate([h_ref[j, 0, :part].astype(jnp.int32).astype(F32) for j in range(2)], axis=0)
    scale = jnp.concatenate([scale_ref[j, 0] for j in range(2)], axis=0)
    h_high, h_low = split(h)
    row = lax.broadcasted_iota(jnp.int32, (rows, wide), 0) + pl.program_id(0) * rows
    for k in range(4):
        cols = pl.ds(pl.multiple_of(((scalars[1] + 4 - k) % 4) * wide, wide), wide)
        update = mm(h_high, high_ref[k]) + (mm(h_high, low_ref[k]) + mm(h_low, high_ref[k]))
        update = update * scale * factor_ref[k, 0:1]
        base = base_ref[:, cols].astype(F32)
        out_ref[:, cols] = jnp.where(row >= scalars[0], base - update, base).astype(BF16)


def apply_update(scalars, panel, scales, errors, base):
    rows, cols = 2 * (panel.shape[2] - 16), base.shape[1]
    wide = cols // 4
    whole = pl.BlockSpec((BLK + 16, wide), lambda i, s: (0, 0))
    stripe = pl.BlockSpec((rows, cols), lambda i, s: (i, 0))
    return pl.pallas_call(
        update_kernel,
        grid_spec=pltpu.PrefetchScalarGridSpec(
            num_scalar_prefetch=1,
            grid=(base.shape[0] // rows,),
            in_specs=[
                pl.BlockSpec((2, 1, rows // 2 + 16, BLK), lambda i, s: (i % 2, i // 2, 0, 0)),
                pl.BlockSpec((2, 1, rows // 2, 1), lambda i, s: (i % 2, i // 2, 0, 0)),
                whole,
                whole,
                whole,
                whole,
                stripe,
            ],
            out_specs=stripe,
            scratch_shapes=[
                pltpu.VMEM((4, BLK, wide), BF16),
                pltpu.VMEM((4, BLK, wide), BF16),
                pltpu.VMEM((4, 16, wide), F32),
            ],
        ),
        out_shape=jax.ShapeDtypeStruct(base.shape, BF16),
        compiler_params=pltpu.CompilerParams(vmem_limit_bytes=32 << 20),
        cost_estimate=pl.CostEstimate(
            flops=6 * base.shape[0] * BLK * cols,
            bytes_accessed=base.shape[0] * cols * 6 + BLK * cols * 2,
            transcendentals=0,
        ),
        name="apply_update",
    )(scalars, panel, scales, *errors, base)


def local(activations, weights, codes, scale_index, scale_table, inverse_block, block_index):
    y, core = lax.axis_index("y"), lax.axis_index("core")
    xl, z, xh = (lax.axis_index(a) for a in PLANE)
    x = 2 * xh + xl
    tile = lax.axis_index(PLANE)
    shard_rows = weights.shape[0]
    tile_units = shard_rows // UNIT
    token_total = activations.shape[0] * 8
    first_unit = block_index[0] * UNITS
    units = first_unit + jnp.arange(UNITS, dtype=jnp.int32)
    owner = units // tile_units
    x_owner, z_owner = 2 * (owner % 2), (owner // 2) % 8
    distance = (z - z_owner) % 8
    from_low = x_owner == jnp.where(x % 2 == 0, x, (x + 3) % 4)

    own_rows = inverse_block.shape[0] // 2
    inverse_part = lax.dynamic_slice_in_dim(inverse_block, core * own_rows, own_rows, 0)
    inverse_part, activations = lax.optimization_barrier((inverse_part, activations))
    inverse = lax.all_gather(inverse_part, ("xh", "xl", "z", "core"), axis=0)
    inverse = inverse.reshape(BLK, BLK)

    index = jnp.clip(units - tile * tile_units, 0, tile_units - 1)
    picks = jnp.append(index, x)
    x_pieces = pick(activations, 1, picks, "pick_columns")
    w_pieces = pick(weights, 0, picks, "pick_rows")

    half = shard_rows // 2
    x_mine = lax.dynamic_slice_in_dim(activations, core * half, half, 1)
    x_theirs = lax.dynamic_slice_in_dim(activations, (1 - core) * half, half, 1)
    x_other = ring("core", 2, 1, x_theirs)
    x_low = jnp.where(core == 0, x_mine, x_other)
    x_high = jnp.where(core == 0, x_other, x_mine)
    x_rows = jnp.concatenate(
        [v[128 * p : 128 * (p + 1)] for p in range(4) for v in (x_low, x_high)], axis=0
    ).T

    lanes = lambda v: jnp.repeat(v, UNIT)[None, :]
    sublanes = lambda v: jnp.repeat(v, UNIT)[:, None]
    x_piece = scatter_x(x_pieces, x, lanes(from_low))
    w_piece = scatter_x(w_pieces, x, sublanes(from_low))
    x_piece, x_rows = reach_far(x_piece, lanes(distance), (x_rows,))
    x_piece = reach_near(x_piece, lanes(distance))
    x_piece, w_piece = lax.optimization_barrier((x_piece, w_piece))

    x_block = lax.all_gather(
        x_piece.astype(jnp.float16), ("xh", "xl", "core"), axis=0, tiled=True
    ).astype(BF16)

    partial_panel = lax.dot_general(
        x_rows, x_block, (((1,), (0,)), ((), ())), preferred_element_type=F32
    )
    w_piece, partial_panel = reach_far(w_piece, sublanes(distance), (partial_panel,))
    w_piece = reach_near(w_piece, sublanes(distance))
    quarter = half // 4
    parts = partial_panel.reshape(4, quarter, BLK)
    message = quantize(parts)
    message, codes, scale_index = lax.optimization_barrier((message, codes, scale_index))
    total = lax.dynamic_index_in_dim(parts, y, 0, False)
    for shift in (1, 3, 2):
        sent = lax.dynamic_index_in_dim(message, (y + shift) % 4, 0, False)
        total = total + dequantize(ring("y", 4, shift, sent))
    chosen = (scale_index[:, :, None] == jnp.arange(LEVELS, dtype=jnp.int32)).astype(F32)
    group_scale = jnp.sum(chosen * scale_table, axis=2)
    quantized = jnp.repeat(group_scale, GROUP, axis=0) * (codes.astype(F32) - 7.5)

    wide = w_piece.shape[1]
    own_columns = lax.dynamic_slice_in_dim(quantized, x * wide, wide, 1)
    error = quantize_columns(block_error(inverse, w_piece, own_columns))
    total, error = lax.optimization_barrier((total, error))
    panel = lax.all_gather(quantize(total), ("y", "core"), axis=0)
    panel = panel.reshape(4, 2, quarter + 16, BLK)
    scales = scales_of(panel) * (2.0 / token_total)

    errors = [error]
    for shift in (1, 2, 3):
        errors.append(lax.ppermute(error, PLANE, plane_pairs(range(4), shift)))

    first_local = block_index[0] * BLK - tile * shard_rows
    padded = jnp.pad(quantized.astype(BF16), [(shard_rows, shard_rows), (0, 0)])
    begin = jnp.clip(shard_rows - first_local, 0, BLK + shard_rows)
    quant_rows = lax.dynamic_slice_in_dim(padded, begin, shard_rows, 0)
    row = jnp.arange(shard_rows, dtype=jnp.int32)[:, None] - first_local
    base = jnp.where((row >= 0) & (row < BLK), quant_rows, weights)
    scalars = jnp.stack([first_local + BLK, x])
    return apply_update(scalars, panel, scales, errors, base)


def solution(mesh):
    cube = Mesh(mesh.devices.reshape(4, 2, 2, 8, 2), ("y", "core") + PLANE)
    return jax.shard_map(
        local,
        mesh=cube,
        in_specs=(
            P(("y", "core"), PLANE),
            P(PLANE, ("y", "core")),
            P(None, ("y", "core")),
            P(None, ("y", "core")),
            P(),
            P(PLANE, None),
            P(),
        ),
        out_specs=P(PLANE, ("y", "core")),
        check_vma=False,
    )
```

```python
import functools
import jax
import jax.numpy as jnp
from jax import lax
from jax.experimental import pallas as pl
from jax.experimental.pallas import tpu as pltpu
from jax.sharding import Mesh, PartitionSpec as P

BLK = 1024
GROUP = 128
LEVELS = 16
UNIT = 128
UNITS = BLK // UNIT
STEPS_PER_OCTAVE = 128.0
F32, BF16, S16 = jnp.float32, jnp.bfloat16, jnp.int16
PLANE = ("xl", "z", "xh")


def tile_at(x, z):
    return (x % 2) * 16 + (z % 8) * 2 + (x % 4) // 2


def ring(axis, size, shift, value):
    return lax.ppermute(value, axis, [(i, (i + shift) % size) for i in range(size)])


def pick_kernel(rows, cols, scalars, src_ref, *out_refs):
    x = scalars[UNITS]
    for k, out_ref in enumerate(out_refs):
        p = (x + k) % 4
        if rows is not None:
            out_ref[...] = src_ref[pl.ds(pl.multiple_of(p * rows, rows), rows), :]
        else:
            out_ref[...] = src_ref[:, pl.ds(pl.multiple_of(p * cols, cols), cols)]


def pick(source, along, scalars, name):
    other = source.shape[1 - along]
    part = other // 4
    if along == 1:
        in_spec = pl.BlockSpec((other, UNIT), lambda j, u: (0, u[j]))
        out_spec = pl.BlockSpec((part, UNIT), lambda j, u: (0, j))
        shape, rows, cols = (part, BLK), part, None
    else:
        in_spec = pl.BlockSpec((UNIT, other), lambda j, u: (u[j], 0))
        out_spec = pl.BlockSpec((UNIT, part), lambda j, u: (j, 0))
        shape, rows, cols = (BLK, part), None, part
    return pl.pallas_call(
        functools.partial(pick_kernel, rows, cols),
        grid_spec=pltpu.PrefetchScalarGridSpec(
            num_scalar_prefetch=1, grid=(UNITS,), in_specs=[in_spec], out_specs=[out_spec] * 4
        ),
        out_shape=[jax.ShapeDtypeStruct(shape, BF16)] * 4,
        name=name,
    )(scalars, source)


def plane_pairs(columns, shift):
    return [(tile_at(s, z), tile_at(s + shift, z)) for s in columns for z in range(8)]


def scatter_x(pieces, x, from_low):
    own, *others = pieces
    up, across, down = (
        lax.ppermute(piece, PLANE, plane_pairs((0, 2), shift))
        for shift, piece in zip((1, 2, 3), others)
    )
    even = x % 2 == 0
    near = jnp.where(even, own, up)
    far = jnp.where(even, across, down)
    return jnp.where(from_low, near, far)


def reach_far(piece, distance, beside=()):
    up, down = ring("z", 8, 3, piece), ring("z", 8, -3, piece)
    up, down, *beside = lax.optimization_barrier((up, down, *beside))
    return jnp.where(distance == 3, up, jnp.where(distance == 5, down, piece)), *beside


def reach_near(piece, distance):
    up, down = ring("z", 8, 1, piece), ring("z", 8, -1, piece)
    from_below = (distance == 1) | (distance == 4) | (distance == 6)
    from_above = (distance == 7) | (distance == 2)
    return jnp.where(from_below, up, jnp.where(from_above, down, piece))


def quantize(values):
    rows = values.shape[-2]
    top = jnp.max(jnp.abs(values), axis=-1, keepdims=True)
    level = jnp.floor(jnp.log2(32700.0 / jnp.maximum(top, 1e-25)) * STEPS_PER_OCTAVE)
    scaled = jnp.round(values * jnp.exp2(level / STEPS_PER_OCTAVE)).astype(jnp.int32).astype(S16)
    levels = jnp.swapaxes(level, -1, -2).astype(jnp.int32).astype(S16)
    widths = [(0, 0)] * (values.ndim - 2) + [(0, 15), (0, values.shape[-1] - rows)]
    return jnp.concatenate([scaled, jnp.pad(levels, widths)], axis=-2)


def scales_of(message):
    rows = message.shape[-2] - 16
    level = message[..., rows : rows + 1, :rows].astype(F32)
    return jnp.swapaxes(jnp.exp2(-level / STEPS_PER_OCTAVE), -1, -2)


def dequantize(message):
    return message[..., :-16, :].astype(F32) * scales_of(message)


def split(values):
    high = values.astype(BF16)
    return high, (values - high.astype(F32)).astype(BF16)


def mm(a, b):
    return jnp.dot(a, b, preferred_element_type=F32)


def error_kernel(inv_ref, w_ref, q_ref, out_ref):
    inv_high, inv_low = split(inv_ref[...])
    dev_high, dev_low = split(w_ref[...].astype(F32) - q_ref[...])
    error = mm(inv_high, dev_high) + (mm(inv_high, dev_low) + mm(inv_low, dev_high))
    i = pl.program_id(0)
    first = ((i % 2) * 16 + i // 2) * 32
    for z in range(8):
        at = pl.multiple_of(first + z * 64, 32)
        out_ref[pl.ds(at, 32), :] = error[z * 32 : (z + 1) * 32]


def block_error(inverse, w_piece, quantized):
    wide = w_piece.shape[1]
    whole = pl.BlockSpec((BLK, wide), lambda i: (0, 0))
    return pl.pallas_call(
        error_kernel,
        grid=(4,),
        in_specs=[pl.BlockSpec((BLK // 4, BLK), lambda i: (i, 0)), whole, whole],
        out_specs=whole,
        out_shape=jax.ShapeDtypeStruct((BLK, wide), F32),
        compiler_params=pltpu.CompilerParams(vmem_limit_bytes=32 << 20),
        cost_estimate=pl.CostEstimate(
            flops=6 * BLK * BLK * wide, bytes_accessed=BLK * BLK * 4, transcendentals=0
        ),
        name="block_error",
    )(inverse, w_piece, quantized)


def quantize_columns(error):
    top = jnp.max(jnp.abs(error), axis=0, keepdims=True)
    level = jnp.floor(jnp.log2(32700.0 / jnp.maximum(top, 1e-25)) * STEPS_PER_OCTAVE)
    scaled = jnp.round(error * jnp.exp2(level / STEPS_PER_OCTAVE))
    levels = jnp.broadcast_to(level, (16, error.shape[1]))
    return jnp.concatenate([scaled, levels], axis=0).astype(jnp.int32).astype(S16)


def update_kernel(scalars, h_ref, scale_ref, e0, e1, e2, e3, base_ref, out_ref, high_ref, low_ref, factor_ref):
    rows, wide = out_ref.shape[0], e0.shape[1]

    @pl.when(pl.program_id(0) == 0)
    def _():
        for k, e in enumerate((e0, e1, e2, e3)):
            high_ref[k], low_ref[k] = split(e[:BLK].astype(jnp.int32).astype(F32))
            level = e[BLK : BLK + 16].astype(jnp.int32).astype(F32)
            factor_ref[k] = jnp.exp2(level * (-1.0 / STEPS_PER_OCTAVE))

    part = rows // 2
    h = jnp.concatenate([h_ref[j, 0, :part].astype(jnp.int32).astype(F32) for j in range(2)], axis=0)
    scale = jnp.concatenate([scale_ref[j, 0] for j in range(2)], axis=0)
    h_high, h_low = split(h)
    row = lax.broadcasted_iota(jnp.int32, (rows, wide), 0) + pl.program_id(0) * rows
    for k in range(4):
        cols = pl.ds(pl.multiple_of(((scalars[1] + 4 - k) % 4) * wide, wide), wide)
        update = mm(h_high, high_ref[k]) + (mm(h_high, low_ref[k]) + mm(h_low, high_ref[k]))
        update = update * scale * factor_ref[k, 0:1]
        base = base_ref[:, cols].astype(F32)
        out_ref[:, cols] = jnp.where(row >= scalars[0], base - update, base).astype(BF16)


def apply_update(scalars, panel, scales, errors, base):
    rows, cols = 2 * (panel.shape[2] - 16), base.shape[1]
    wide = cols // 4
    whole = pl.BlockSpec((BLK + 16, wide), lambda i, s: (0, 0))
    stripe = pl.BlockSpec((rows, cols), lambda i, s: (i, 0))
    return pl.pallas_call(
        update_kernel,
        grid_spec=pltpu.PrefetchScalarGridSpec(
            num_scalar_prefetch=1,
            grid=(base.shape[0] // rows,),
            in_specs=[
                pl.BlockSpec((2, 1, rows // 2 + 16, BLK), lambda i, s: (i % 2, i // 2, 0, 0)),
                pl.BlockSpec((2, 1, rows // 2, 1), lambda i, s: (i % 2, i // 2, 0, 0)),
                whole,
                whole,
                whole,
                whole,
                stripe,
            ],
            out_specs=stripe,
            scratch_shapes=[
                pltpu.VMEM((4, BLK, wide), BF16),
                pltpu.VMEM((4, BLK, wide), BF16),
                pltpu.VMEM((4, 16, wide), F32),
            ],
        ),
        out_shape=jax.ShapeDtypeStruct(base.shape, BF16),
        compiler_params=pltpu.CompilerParams(vmem_limit_bytes=32 << 20),
        cost_estimate=pl.CostEstimate(
            flops=6 * base.shape[0] * BLK * cols,
            bytes_accessed=base.shape[0] * cols * 6 + BLK * cols * 2,
            transcendentals=0,
        ),
        name="apply_update",
    )(scalars, panel, scales, *errors, base)


def local(activations, weights, codes, scale_index, scale_table, inverse_block, block_index):
    y, core = lax.axis_index("y"), lax.axis_index("core")
    xl, z, xh = (lax.axis_index(a) for a in PLANE)
    x = 2 * xh + xl
    tile = lax.axis_index(PLANE)
    shard_rows = weights.shape[0]
    tile_units = shard_rows // UNIT
    token_total = activations.shape[0] * 8
    first_unit = block_index[0] * UNITS
    units = first_unit + jnp.arange(UNITS, dtype=jnp.int32)
    owner = units // tile_units
    x_owner, z_owner = 2 * (owner % 2), (owner // 2) % 8
    distance = (z - z_owner) % 8
    from_low = x_owner == jnp.where(x % 2 == 0, x, (x + 3) % 4)

    own_rows = inverse_block.shape[0] // 2
    inverse_part = lax.dynamic_slice_in_dim(inverse_block, core * own_rows, own_rows, 0)
    inverse_part, activations = lax.optimization_barrier((inverse_part, activations))
    inverse = lax.all_gather(inverse_part, ("xh", "xl", "z", "core"), axis=0)
    inverse = inverse.reshape(BLK, BLK)

    index = jnp.clip(units - tile * tile_units, 0, tile_units - 1)
    picks = jnp.append(index, x)
    x_pieces = pick(activations, 1, picks, "pick_columns")
    w_pieces = pick(weights, 0, picks, "pick_rows")

    half = shard_rows // 2
    x_mine = lax.dynamic_slice_in_dim(activations, core * half, half, 1)
    x_theirs = lax.dynamic_slice_in_dim(activations, (1 - core) * half, half, 1)
    x_other = ring("core", 2, 1, x_theirs)
    x_low = jnp.where(core == 0, x_mine, x_other)
    x_high = jnp.where(core == 0, x_other, x_mine)
    x_rows = jnp.concatenate(
        [v[128 * p : 128 * (p + 1)] for p in range(4) for v in (x_low, x_high)], axis=0
    ).T

    lanes = lambda v: jnp.repeat(v, UNIT)[None, :]
    sublanes = lambda v: jnp.repeat(v, UNIT)[:, None]
    x_piece = scatter_x(x_pieces, x, lanes(from_low))
    w_piece = scatter_x(w_pieces, x, sublanes(from_low))
    x_piece, x_rows = reach_far(x_piece, lanes(distance), (x_rows,))
    x_piece = reach_near(x_piece, lanes(distance))
    x_piece, w_piece = lax.optimization_barrier((x_piece, w_piece))

    x_block = lax.all_gather(
        x_piece.astype(jnp.float16), ("xh", "xl", "core"), axis=0, tiled=True
    ).astype(BF16)

    partial_panel = lax.dot_general(
        x_rows, x_block, (((1,), (0,)), ((), ())), preferred_element_type=F32
    )
    w_piece, = reach_far(w_piece, sublanes(distance))
    w_piece = reach_near(w_piece, sublanes(distance))
    quarter = half // 4
    parts = partial_panel.reshape(4, quarter, BLK)
    message = quantize(parts)
    message, codes, scale_index = lax.optimization_barrier((message, codes, scale_index))
    total = lax.dynamic_index_in_dim(parts, y, 0, False)
    for shift in (1, 3, 2):
        sent = lax.dynamic_index_in_dim(message, (y + shift) % 4, 0, False)
        got = ring("y", 4, shift, sent)
        if shift == 1:
            got, inverse = lax.optimization_barrier((got, inverse))
        total = total + dequantize(got)
    chosen = (scale_index[:, :, None] == jnp.arange(LEVELS, dtype=jnp.int32)).astype(F32)
    group_scale = jnp.sum(chosen * scale_table, axis=2)
    quantized = jnp.repeat(group_scale, GROUP, axis=0) * (codes.astype(F32) - 7.5)

    wide = w_piece.shape[1]
    own_columns = lax.dynamic_slice_in_dim(quantized, x * wide, wide, 1)
    error = quantize_columns(block_error(inverse, w_piece, own_columns))
    total, error = lax.optimization_barrier((total, error))
    panel = lax.all_gather(quantize(total), ("y", "core"), axis=0)
    panel = panel.reshape(4, 2, quarter + 16, BLK)
    scales = scales_of(panel) * (2.0 / token_total)

    errors = [error]
    for shift in (1, 2, 3):
        errors.append(lax.ppermute(error, PLANE, plane_pairs(range(4), shift)))

    first_local = block_index[0] * BLK - tile * shard_rows
    padded = jnp.pad(quantized.astype(BF16), [(shard_rows, shard_rows), (0, 0)])
    begin = jnp.clip(shard_rows - first_local, 0, BLK + shard_rows)
    quant_rows = lax.dynamic_slice_in_dim(padded, begin, shard_rows, 0)
    row = jnp.arange(shard_rows, dtype=jnp.int32)[:, None] - first_local
    base = jnp.where((row >= 0) & (row < BLK), quant_rows, weights)
    scalars = jnp.stack([first_local + BLK, x])
    return apply_update(scalars, panel, scales, errors, base)


def solution(mesh):
    cube = Mesh(mesh.devices.reshape(4, 2, 2, 8, 2), ("y", "core") + PLANE)
    return jax.shard_map(
        local,
        mesh=cube,
        in_specs=(
            P(("y", "core"), PLANE),
            P(PLANE, ("y", "core")),
            P(None, ("y", "core")),
            P(None, ("y", "core")),
            P(),
            P(PLANE, None),
            P(),
        ),
        out_specs=P(PLANE, ("y", "core")),
        check_vma=False,
    )
```

```python
import functools
import jax
import jax.numpy as jnp
from jax import lax
from jax.experimental import pallas as pl
from jax.experimental.pallas import tpu as pltpu
from jax.sharding import Mesh, PartitionSpec as P

BLK = 1024
GROUP = 128
LEVELS = 16
UNIT = 128
UNITS = BLK // UNIT
STEPS_PER_OCTAVE = 128.0
F32, BF16, S16 = jnp.float32, jnp.bfloat16, jnp.int16
PLANE = ("xl", "z", "xh")


def tile_at(x, z):
    return (x % 2) * 16 + (z % 8) * 2 + (x % 4) // 2


def ring(axis, size, shift, value):
    return lax.ppermute(value, axis, [(i, (i + shift) % size) for i in range(size)])


def pick_kernel(rows, cols, scalars, src_ref, *out_refs):
    x = scalars[UNITS]
    for k, out_ref in enumerate(out_refs):
        p = (x + k) % 4
        if rows is not None:
            out_ref[...] = src_ref[pl.ds(pl.multiple_of(p * rows, rows), rows), :]
        else:
            out_ref[...] = src_ref[:, pl.ds(pl.multiple_of(p * cols, cols), cols)]


def pick(source, along, scalars, name):
    other = source.shape[1 - along]
    part = other // 4
    if along == 1:
        in_spec = pl.BlockSpec((other, UNIT), lambda j, u: (0, u[j]))
        out_spec = pl.BlockSpec((part, UNIT), lambda j, u: (0, j))
        shape, rows, cols = (part, BLK), part, None
    else:
        in_spec = pl.BlockSpec((UNIT, other), lambda j, u: (u[j], 0))
        out_spec = pl.BlockSpec((UNIT, part), lambda j, u: (j, 0))
        shape, rows, cols = (BLK, part), None, part
    return pl.pallas_call(
        functools.partial(pick_kernel, rows, cols),
        grid_spec=pltpu.PrefetchScalarGridSpec(
            num_scalar_prefetch=1, grid=(UNITS,), in_specs=[in_spec], out_specs=[out_spec] * 4
        ),
        out_shape=[jax.ShapeDtypeStruct(shape, BF16)] * 4,
        name=name,
    )(scalars, source)


def plane_pairs(columns, shift):
    return [(tile_at(s, z), tile_at(s + shift, z)) for s in columns for z in range(8)]


def scatter_x(pieces, x, from_low):
    own, *others = pieces
    up, across, down = (
        lax.ppermute(piece, PLANE, plane_pairs((0, 2), shift))
        for shift, piece in zip((1, 2, 3), others)
    )
    even = x % 2 == 0
    near = jnp.where(even, own, up)
    far = jnp.where(even, across, down)
    return jnp.where(from_low, near, far)


def reach_far(piece, distance, beside=()):
    up, down = ring("z", 8, 3, piece), ring("z", 8, -3, piece)
    up, down, *beside = lax.optimization_barrier((up, down, *beside))
    return jnp.where(distance == 3, up, jnp.where(distance == 5, down, piece)), *beside


def reach_near(piece, distance):
    up, down = ring("z", 8, 1, piece), ring("z", 8, -1, piece)
    from_below = (distance == 1) | (distance == 4) | (distance == 6)
    from_above = (distance == 7) | (distance == 2)
    return jnp.where(from_below, up, jnp.where(from_above, down, piece))


def quantize(values):
    rows = values.shape[-2]
    top = jnp.max(jnp.abs(values), axis=-1, keepdims=True)
    level = jnp.floor(jnp.log2(32700.0 / jnp.maximum(top, 1e-25)) * STEPS_PER_OCTAVE)
    scaled = jnp.round(values * jnp.exp2(level / STEPS_PER_OCTAVE)).astype(jnp.int32).astype(S16)
    levels = jnp.swapaxes(level, -1, -2).astype(jnp.int32).astype(S16)
    widths = [(0, 0)] * (values.ndim - 2) + [(0, 15), (0, values.shape[-1] - rows)]
    return jnp.concatenate([scaled, jnp.pad(levels, widths)], axis=-2)


def scales_of(message):
    rows = message.shape[-2] - 16
    level = message[..., rows : rows + 1, :rows].astype(F32)
    return jnp.swapaxes(jnp.exp2(-level / STEPS_PER_OCTAVE), -1, -2)


def dequantize(message):
    return message[..., :-16, :].astype(F32) * scales_of(message)


def split(values):
    high = values.astype(BF16)
    return high, (values - high.astype(F32)).astype(BF16)


def mm(a, b):
    return jnp.dot(a, b, preferred_element_type=F32)


def error_kernel(inv_ref, w_ref, q_ref, out_ref):
    inv_high, inv_low = split(inv_ref[...])
    dev_high, dev_low = split(w_ref[...].astype(F32) - q_ref[...])
    error = mm(inv_high, dev_high) + (mm(inv_high, dev_low) + mm(inv_low, dev_high))
    i = pl.program_id(0)
    first = ((i % 2) * 16 + i // 2) * 32
    for z in range(8):
        at = pl.multiple_of(first + z * 64, 32)
        out_ref[pl.ds(at, 32), :] = error[z * 32 : (z + 1) * 32]


def block_error(inverse, w_piece, quantized):
    wide = w_piece.shape[1]
    whole = pl.BlockSpec((BLK, wide), lambda i: (0, 0))
    return pl.pallas_call(
        error_kernel,
        grid=(4,),
        in_specs=[pl.BlockSpec((BLK // 4, BLK), lambda i: (i, 0)), whole, whole],
        out_specs=whole,
        out_shape=jax.ShapeDtypeStruct((BLK, wide), F32),
        compiler_params=pltpu.CompilerParams(vmem_limit_bytes=32 << 20),
        cost_estimate=pl.CostEstimate(
            flops=6 * BLK * BLK * wide, bytes_accessed=BLK * BLK * 4, transcendentals=0
        ),
        name="block_error",
    )(inverse, w_piece, quantized)


def quantize_columns(error):
    top = jnp.max(jnp.abs(error), axis=0, keepdims=True)
    level = jnp.floor(jnp.log2(32700.0 / jnp.maximum(top, 1e-25)) * STEPS_PER_OCTAVE)
    scaled = jnp.round(error * jnp.exp2(level / STEPS_PER_OCTAVE))
    levels = jnp.broadcast_to(level, (16, error.shape[1]))
    return jnp.concatenate([scaled, levels], axis=0).astype(jnp.int32).astype(S16)


def update_kernel(scalars, h_ref, scale_ref, e0, e1, e2, e3, base_ref, out_ref, high_ref, low_ref, factor_ref):
    rows, wide = out_ref.shape[0], e0.shape[1]

    @pl.when(pl.program_id(0) == 0)
    def _():
        for k, e in enumerate((e0, e1, e2, e3)):
            high_ref[k], low_ref[k] = split(e[:BLK].astype(jnp.int32).astype(F32))
            level = e[BLK : BLK + 16].astype(jnp.int32).astype(F32)
            factor_ref[k] = jnp.exp2(level * (-1.0 / STEPS_PER_OCTAVE))

    part = rows // 2
    h = jnp.concatenate([h_ref[j, 0, :part].astype(jnp.int32).astype(F32) for j in range(2)], axis=0)
    scale = jnp.concatenate([scale_ref[j, 0] for j in range(2)], axis=0)
    h_high, h_low = split(h)
    row = lax.broadcasted_iota(jnp.int32, (rows, wide), 0) + pl.program_id(0) * rows
    for k in range(4):
        cols = pl.ds(pl.multiple_of(((scalars[1] + 4 - k) % 4) * wide, wide), wide)
        update = mm(h_high, high_ref[k]) + (mm(h_high, low_ref[k]) + mm(h_low, high_ref[k]))
        update = update * scale * factor_ref[k, 0:1]
        base = base_ref[:, cols].astype(F32)
        out_ref[:, cols] = jnp.where(row >= scalars[0], base - update, base).astype(BF16)


def apply_update(scalars, panel, scales, errors, base):
    rows, cols = 2 * (panel.shape[2] - 16), base.shape[1]
    wide = cols // 4
    whole = pl.BlockSpec((BLK + 16, wide), lambda i, s: (0, 0))
    stripe = pl.BlockSpec((rows, cols), lambda i, s: (i, 0))
    return pl.pallas_call(
        update_kernel,
        grid_spec=pltpu.PrefetchScalarGridSpec(
            num_scalar_prefetch=1,
            grid=(base.shape[0] // rows,),
            in_specs=[
                pl.BlockSpec((2, 1, rows // 2 + 16, BLK), lambda i, s: (i % 2, i // 2, 0, 0)),
                pl.BlockSpec((2, 1, rows // 2, 1), lambda i, s: (i % 2, i // 2, 0, 0)),
                whole,
                whole,
                whole,
                whole,
                stripe,
            ],
            out_specs=stripe,
            scratch_shapes=[
                pltpu.VMEM((4, BLK, wide), BF16),
                pltpu.VMEM((4, BLK, wide), BF16),
                pltpu.VMEM((4, 16, wide), F32),
            ],
        ),
        out_shape=jax.ShapeDtypeStruct(base.shape, BF16),
        compiler_params=pltpu.CompilerParams(vmem_limit_bytes=32 << 20),
        cost_estimate=pl.CostEstimate(
            flops=6 * base.shape[0] * BLK * cols,
            bytes_accessed=base.shape[0] * cols * 6 + BLK * cols * 2,
            transcendentals=0,
        ),
        name="apply_update",
    )(scalars, panel, scales, *errors, base)


def local(activations, weights, codes, scale_index, scale_table, inverse_block, block_index):
    y, core = lax.axis_index("y"), lax.axis_index("core")
    xl, z, xh = (lax.axis_index(a) for a in PLANE)
    x = 2 * xh + xl
    tile = lax.axis_index(PLANE)
    shard_rows = weights.shape[0]
    tile_units = shard_rows // UNIT
    token_total = activations.shape[0] * 8
    first_unit = block_index[0] * UNITS
    units = first_unit + jnp.arange(UNITS, dtype=jnp.int32)
    owner = units // tile_units
    x_owner, z_owner = 2 * (owner % 2), (owner // 2) % 8
    distance = (z - z_owner) % 8
    from_low = x_owner == jnp.where(x % 2 == 0, x, (x + 3) % 4)

    own_rows = inverse_block.shape[0] // 2
    inverse_part = lax.dynamic_slice_in_dim(inverse_block, core * own_rows, own_rows, 0)
    inverse_part, activations = lax.optimization_barrier((inverse_part, activations))
    inverse = lax.all_gather(inverse_part, ("xh", "xl", "z", "core"), axis=0)
    inverse = inverse.reshape(BLK, BLK)

    index = jnp.clip(units - tile * tile_units, 0, tile_units - 1)
    picks = jnp.append(index, x)
    x_pieces = pick(activations, 1, picks, "pick_columns")
    w_pieces = pick(weights, 0, picks, "pick_rows")

    half = shard_rows // 2
    x_mine = lax.dynamic_slice_in_dim(activations, core * half, half, 1)
    x_theirs = lax.dynamic_slice_in_dim(activations, (1 - core) * half, half, 1)
    x_other = ring("core", 2, 1, x_theirs)
    x_low = jnp.where(core == 0, x_mine, x_other)
    x_high = jnp.where(core == 0, x_other, x_mine)
    x_rows = jnp.concatenate(
        [v[128 * p : 128 * (p + 1)] for p in range(4) for v in (x_low, x_high)], axis=0
    ).T

    lanes = lambda v: jnp.repeat(v, UNIT)[None, :]
    sublanes = lambda v: jnp.repeat(v, UNIT)[:, None]
    x_piece = scatter_x(x_pieces, x, lanes(from_low))
    w_piece = scatter_x(w_pieces, x, sublanes(from_low))
    x_piece, x_rows = reach_far(x_piece, lanes(distance), (x_rows,))
    x_piece, w_piece = lax.optimization_barrier((x_piece, w_piece))
    x_piece = reach_near(x_piece, lanes(distance))

    x_block = lax.all_gather(
        x_piece.astype(jnp.float16), ("xh", "xl", "core"), axis=0, tiled=True
    ).astype(BF16)

    partial_panel = lax.dot_general(
        x_rows, x_block, (((1,), (0,)), ((), ())), preferred_element_type=F32
    )
    w_piece, inverse = reach_far(w_piece, sublanes(distance), (inverse,))
    w_piece = reach_near(w_piece, sublanes(distance))
    quarter = half // 4
    parts = partial_panel.reshape(4, quarter, BLK)
    message = quantize(parts)
    message, codes, scale_index = lax.optimization_barrier((message, codes, scale_index))
    total = lax.dynamic_index_in_dim(parts, y, 0, False)
    for shift in (1, 3, 2):
        sent = lax.dynamic_index_in_dim(message, (y + shift) % 4, 0, False)
        got = ring("y", 4, shift, sent)
        if shift == 1:
            got, w_piece = lax.optimization_barrier((got, w_piece))
        total = total + dequantize(got)
    chosen = (scale_index[:, :, None] == jnp.arange(LEVELS, dtype=jnp.int32)).astype(F32)
    group_scale = jnp.sum(chosen * scale_table, axis=2)
    quantized = jnp.repeat(group_scale, GROUP, axis=0) * (codes.astype(F32) - 7.5)

    wide = w_piece.shape[1]
    own_columns = lax.dynamic_slice_in_dim(quantized, x * wide, wide, 1)
    error = quantize_columns(block_error(inverse, w_piece, own_columns))
    total, error = lax.optimization_barrier((total, error))
    panel = lax.all_gather(quantize(total), ("y", "core"), axis=0)
    panel = panel.reshape(4, 2, quarter + 16, BLK)
    scales = scales_of(panel) * (2.0 / token_total)

    errors = [error]
    for shift in (1, 2, 3):
        errors.append(lax.ppermute(error, PLANE, plane_pairs(range(4), shift)))

    first_local = block_index[0] * BLK - tile * shard_rows
    padded = jnp.pad(quantized.astype(BF16), [(shard_rows, shard_rows), (0, 0)])
    begin = jnp.clip(shard_rows - first_local, 0, BLK + shard_rows)
    quant_rows = lax.dynamic_slice_in_dim(padded, begin, shard_rows, 0)
    row = jnp.arange(shard_rows, dtype=jnp.int32)[:, None] - first_local
    base = jnp.where((row >= 0) & (row < BLK), quant_rows, weights)
    scalars = jnp.stack([first_local + BLK, x])
    return apply_update(scalars, panel, scales, errors, base)


def solution(mesh):
    cube = Mesh(mesh.devices.reshape(4, 2, 2, 8, 2), ("y", "core") + PLANE)
    return jax.shard_map(
        local,
        mesh=cube,
        in_specs=(
            P(("y", "core"), PLANE),
            P(PLANE, ("y", "core")),
            P(None, ("y", "core")),
            P(None, ("y", "core")),
            P(),
            P(PLANE, None),
            P(),
        ),
        out_specs=P(PLANE, ("y", "core")),
        check_vma=False,
    )
```

```python
import functools
import jax
import jax.numpy as jnp
from jax import lax
from jax.experimental import pallas as pl
from jax.experimental.pallas import tpu as pltpu
from jax.sharding import Mesh, PartitionSpec as P

BLK = 1024
GROUP = 128
LEVELS = 16
UNIT = 128
UNITS = BLK // UNIT
STEPS_PER_OCTAVE = 128.0
F32, BF16, S16 = jnp.float32, jnp.bfloat16, jnp.int16
PLANE = ("xl", "z", "xh")


def tile_at(x, z):
    return (x % 2) * 16 + (z % 8) * 2 + (x % 4) // 2


def ring(axis, size, shift, value):
    return lax.ppermute(value, axis, [(i, (i + shift) % size) for i in range(size)])


def pick_kernel(rows, cols, scalars, src_ref, *out_refs):
    x = scalars[UNITS]
    for k, out_ref in enumerate(out_refs):
        p = (x + k) % 4
        if rows is not None:
            out_ref[...] = src_ref[pl.ds(pl.multiple_of(p * rows, rows), rows), :]
        else:
            out_ref[...] = src_ref[:, pl.ds(pl.multiple_of(p * cols, cols), cols)]


def pick(source, along, scalars, name):
    other = source.shape[1 - along]
    part = other // 4
    if along == 1:
        in_spec = pl.BlockSpec((other, UNIT), lambda j, u: (0, u[j]))
        out_spec = pl.BlockSpec((part, UNIT), lambda j, u: (0, j))
        shape, rows, cols = (part, BLK), part, None
    else:
        in_spec = pl.BlockSpec((UNIT, other), lambda j, u: (u[j], 0))
        out_spec = pl.BlockSpec((UNIT, part), lambda j, u: (j, 0))
        shape, rows, cols = (BLK, part), None, part
    return pl.pallas_call(
        functools.partial(pick_kernel, rows, cols),
        grid_spec=pltpu.PrefetchScalarGridSpec(
            num_scalar_prefetch=1, grid=(UNITS,), in_specs=[in_spec], out_specs=[out_spec] * 4
        ),
        out_shape=[jax.ShapeDtypeStruct(shape, BF16)] * 4,
        name=name,
    )(scalars, source)


def plane_pairs(columns, shift):
    return [(tile_at(s, z), tile_at(s + shift, z)) for s in columns for z in range(8)]


def scatter_x(pieces, x, from_low):
    own, *others = pieces
    up, across, down = (
        lax.ppermute(piece, PLANE, plane_pairs((0, 2), shift))
        for shift, piece in zip((1, 2, 3), others)
    )
    even = x % 2 == 0
    near = jnp.where(even, own, up)
    far = jnp.where(even, across, down)
    return jnp.where(from_low, near, far)


def reach_far(piece, distance, beside=()):
    up, down = ring("z", 8, 3, piece), ring("z", 8, -3, piece)
    up, down, *beside = lax.optimization_barrier((up, down, *beside))
    return jnp.where(distance == 3, up, jnp.where(distance == 5, down, piece)), *beside


def reach_near(piece, distance):
    up, down = ring("z", 8, 1, piece), ring("z", 8, -1, piece)
    from_below = (distance == 1) | (distance == 4) | (distance == 6)
    from_above = (distance == 7) | (distance == 2)
    return jnp.where(from_below, up, jnp.where(from_above, down, piece))


def quantize(values):
    rows = values.shape[-2]
    top = jnp.max(jnp.abs(values), axis=-1, keepdims=True)
    level = jnp.floor(jnp.log2(32700.0 / jnp.maximum(top, 1e-25)) * STEPS_PER_OCTAVE)
    scaled = jnp.round(values * jnp.exp2(level / STEPS_PER_OCTAVE)).astype(jnp.int32).astype(S16)
    levels = jnp.swapaxes(level, -1, -2).astype(jnp.int32).astype(S16)
    widths = [(0, 0)] * (values.ndim - 2) + [(0, 15), (0, values.shape[-1] - rows)]
    return jnp.concatenate([scaled, jnp.pad(levels, widths)], axis=-2)


def scales_of(message):
    rows = message.shape[-2] - 16
    level = message[..., rows : rows + 1, :rows].astype(F32)
    return jnp.swapaxes(jnp.exp2(-level / STEPS_PER_OCTAVE), -1, -2)


def dequantize(message):
    return message[..., :-16, :].astype(F32) * scales_of(message)


def split(values):
    high = values.astype(BF16)
    return high, (values - high.astype(F32)).astype(BF16)


def mm(a, b):
    return jnp.dot(a, b, preferred_element_type=F32)


def error_kernel(inv_ref, w_ref, q_ref, out_ref):
    inv_high, inv_low = split(inv_ref[...])
    dev_high, dev_low = split(w_ref[...].astype(F32) - q_ref[...])
    error = mm(inv_high, dev_high) + (mm(inv_high, dev_low) + mm(inv_low, dev_high))
    i = pl.program_id(0)
    first = ((i % 2) * 16 + i // 2) * 32
    for z in range(8):
        at = pl.multiple_of(first + z * 64, 32)
        out_ref[pl.ds(at, 32), :] = error[z * 32 : (z + 1) * 32]


def block_error(inverse, w_piece, quantized):
    wide = w_piece.shape[1]
    whole = pl.BlockSpec((BLK, wide), lambda i: (0, 0))
    return pl.pallas_call(
        error_kernel,
        grid=(4,),
        in_specs=[pl.BlockSpec((BLK // 4, BLK), lambda i: (i, 0)), whole, whole],
        out_specs=whole,
        out_shape=jax.ShapeDtypeStruct((BLK, wide), F32),
        compiler_params=pltpu.CompilerParams(vmem_limit_bytes=32 << 20),
        cost_estimate=pl.CostEstimate(
            flops=6 * BLK * BLK * wide, bytes_accessed=BLK * BLK * 4, transcendentals=0
        ),
        name="block_error",
    )(inverse, w_piece, quantized)


def quantize_columns(error):
    top = jnp.max(jnp.abs(error), axis=0, keepdims=True)
    level = jnp.floor(jnp.log2(32700.0 / jnp.maximum(top, 1e-25)) * STEPS_PER_OCTAVE)
    scaled = jnp.round(error * jnp.exp2(level / STEPS_PER_OCTAVE))
    levels = jnp.broadcast_to(level, (16, error.shape[1]))
    return jnp.concatenate([scaled, levels], axis=0).astype(jnp.int32).astype(S16)


def update_kernel(scalars, h_ref, scale_ref, e0, e1, e2, e3, base_ref, out_ref, high_ref, low_ref, factor_ref):
    rows, wide = out_ref.shape[0], e0.shape[1]

    @pl.when(pl.program_id(0) == 0)
    def _():
        for k, e in enumerate((e0, e1, e2, e3)):
            high_ref[k], low_ref[k] = split(e[:BLK].astype(jnp.int32).astype(F32))
            level = e[BLK : BLK + 16].astype(jnp.int32).astype(F32)
            factor_ref[k] = jnp.exp2(level * (-1.0 / STEPS_PER_OCTAVE))

    part = rows // 2
    h = jnp.concatenate([h_ref[j, 0, :part].astype(jnp.int32).astype(F32) for j in range(2)], axis=0)
    scale = jnp.concatenate([scale_ref[j, 0] for j in range(2)], axis=0)
    h_high, h_low = split(h)
    row = lax.broadcasted_iota(jnp.int32, (rows, wide), 0) + pl.program_id(0) * rows
    for k in range(4):
        cols = pl.ds(pl.multiple_of(((scalars[1] + 4 - k) % 4) * wide, wide), wide)
        update = mm(h_high, high_ref[k]) + (mm(h_high, low_ref[k]) + mm(h_low, high_ref[k]))
        update = update * scale * factor_ref[k, 0:1]
        base = base_ref[:, cols].astype(F32)
        out_ref[:, cols] = jnp.where(row >= scalars[0], base - update, base).astype(BF16)


def apply_update(scalars, panel, scales, errors, base):
    rows, cols = 2 * (panel.shape[2] - 16), base.shape[1]
    wide = cols // 4
    whole = pl.BlockSpec((BLK + 16, wide), lambda i, s: (0, 0))
    stripe = pl.BlockSpec((rows, cols), lambda i, s: (i, 0))
    return pl.pallas_call(
        update_kernel,
        grid_spec=pltpu.PrefetchScalarGridSpec(
            num_scalar_prefetch=1,
            grid=(base.shape[0] // rows,),
            in_specs=[
                pl.BlockSpec((2, 1, rows // 2 + 16, BLK), lambda i, s: (i % 2, i // 2, 0, 0)),
                pl.BlockSpec((2, 1, rows // 2, 1), lambda i, s: (i % 2, i // 2, 0, 0)),
                whole,
                whole,
                whole,
                whole,
                stripe,
            ],
            out_specs=stripe,
            scratch_shapes=[
                pltpu.VMEM((4, BLK, wide), BF16),
                pltpu.VMEM((4, BLK, wide), BF16),
                pltpu.VMEM((4, 16, wide), F32),
            ],
        ),
        out_shape=jax.ShapeDtypeStruct(base.shape, BF16),
        compiler_params=pltpu.CompilerParams(vmem_limit_bytes=32 << 20),
        cost_estimate=pl.CostEstimate(
            flops=6 * base.shape[0] * BLK * cols,
            bytes_accessed=base.shape[0] * cols * 6 + BLK * cols * 2,
            transcendentals=0,
        ),
        name="apply_update",
    )(scalars, panel, scales, *errors, base)


def local(activations, weights, codes, scale_index, scale_table, inverse_block, block_index):
    y, core = lax.axis_index("y"), lax.axis_index("core")
    xl, z, xh = (lax.axis_index(a) for a in PLANE)
    x = 2 * xh + xl
    tile = lax.axis_index(PLANE)
    shard_rows = weights.shape[0]
    tile_units = shard_rows // UNIT
    token_total = activations.shape[0] * 8
    first_unit = block_index[0] * UNITS
    units = first_unit + jnp.arange(UNITS, dtype=jnp.int32)
    owner = units // tile_units
    x_owner, z_owner = 2 * (owner % 2), (owner // 2) % 8
    distance = (z - z_owner) % 8
    from_low = x_owner == jnp.where(x % 2 == 0, x, (x + 3) % 4)

    own_rows = inverse_block.shape[0] // 2
    inverse_part = lax.dynamic_slice_in_dim(inverse_block, core * own_rows, own_rows, 0)
    inverse_part, activations = lax.optimization_barrier((inverse_part, activations))
    inverse = lax.all_gather(inverse_part, ("xh", "xl", "z", "core"), axis=0)
    inverse = inverse.reshape(BLK, BLK)

    index = jnp.clip(units - tile * tile_units, 0, tile_units - 1)
    picks = jnp.append(index, x)
    x_pieces = pick(activations, 1, picks, "pick_columns")
    w_pieces = pick(weights, 0, picks, "pick_rows")

    half = shard_rows // 2
    x_mine = lax.dynamic_slice_in_dim(activations, core * half, half, 1)
    x_theirs = lax.dynamic_slice_in_dim(activations, (1 - core) * half, half, 1)
    x_other = ring("core", 2, 1, x_theirs)
    x_low = jnp.where(core == 0, x_mine, x_other)
    x_high = jnp.where(core == 0, x_other, x_mine)
    x_rows = jnp.concatenate(
        [v[128 * p : 128 * (p + 1)] for p in range(4) for v in (x_low, x_high)], axis=0
    ).T

    lanes = lambda v: jnp.repeat(v, UNIT)[None, :]
    sublanes = lambda v: jnp.repeat(v, UNIT)[:, None]
    x_piece = scatter_x(x_pieces, x, lanes(from_low))
    w_piece = scatter_x(w_pieces, x, sublanes(from_low))
    x_piece, x_rows = reach_far(x_piece, lanes(distance), (x_rows,))
    x_piece = reach_near(x_piece, lanes(distance))
    x_piece, w_piece = lax.optimization_barrier((x_piece, w_piece))

    x_block = lax.all_gather(
        x_piece.astype(jnp.float16), ("xh", "xl", "core"), axis=0, tiled=True
    ).astype(BF16)

    partial_panel = lax.dot_general(
        x_rows, x_block, (((1,), (0,)), ((), ())), preferred_element_type=F32
    )
    w_piece, inverse = reach_far(w_piece, sublanes(distance), (inverse,))
    w_piece = reach_near(w_piece, sublanes(distance))
    quarter = half // 4
    parts = partial_panel.reshape(4, quarter, BLK)
    message = quantize(parts)
    message, codes, scale_index = lax.optimization_barrier((message, codes, scale_index))
    total = lax.dynamic_index_in_dim(parts, y, 0, False)
    for shift in (1, 3, 2):
        sent = lax.dynamic_index_in_dim(message, (y + shift) % 4, 0, False)
        got = ring("y", 4, shift, sent)
        if shift == 1:
            got, w_piece = lax.optimization_barrier((got, w_piece))
        total = total + dequantize(got)
    chosen = (scale_index[:, :, None] == jnp.arange(LEVELS, dtype=jnp.int32)).astype(F32)
    group_scale = jnp.sum(chosen * scale_table, axis=2)
    quantized = jnp.repeat(group_scale, GROUP, axis=0) * (codes.astype(F32) - 7.5)

    wide = w_piece.shape[1]
    own_columns = lax.dynamic_slice_in_dim(quantized, x * wide, wide, 1)
    error = quantize_columns(block_error(inverse, w_piece, own_columns))
    total, error = lax.optimization_barrier((total, error))
    panel = lax.all_gather(quantize(total), ("y", "core"), axis=0)
    panel = panel.reshape(4, 2, quarter + 16, BLK)
    scales = scales_of(panel) * (2.0 / token_total)

    errors = [error]
    for shift in (1, 2, 3):
        errors.append(lax.ppermute(error, PLANE, plane_pairs(range(4), shift)))

    first_local = block_index[0] * BLK - tile * shard_rows
    padded = jnp.pad(quantized.astype(BF16), [(shard_rows, shard_rows), (0, 0)])
    begin = jnp.clip(shard_rows - first_local, 0, BLK + shard_rows)
    quant_rows = lax.dynamic_slice_in_dim(padded, begin, shard_rows, 0)
    row = jnp.arange(shard_rows, dtype=jnp.int32)[:, None] - first_local
    base = jnp.where((row >= 0) & (row < BLK), quant_rows, weights)
    scalars = jnp.stack([first_local + BLK, x])
    return apply_update(scalars, panel, scales, errors, base)


def solution(mesh):
    cube = Mesh(mesh.devices.reshape(4, 2, 2, 8, 2), ("y", "core") + PLANE)
    return jax.shard_map(
        local,
        mesh=cube,
        in_specs=(
            P(("y", "core"), PLANE),
            P(PLANE, ("y", "core")),
            P(None, ("y", "core")),
            P(None, ("y", "core")),
            P(),
            P(PLANE, None),
            P(),
        ),
        out_specs=P(PLANE, ("y", "core")),
        check_vma=False,
    )
```
